512 devices in a mesh: replica: 16 (over x, y_lo), fsdp: 32 (over z, y_hi, core).
Axes of the slice: x: 4, y: 8 (y_hi: 2, y_lo: 4; y = y_hi * 4 + y_lo), z: 8, core: 2. Of those that a mesh axis runs over, the one named last changes fastest.
Arguments:
- tokens: bfloat16 [16, 4096, 256], P('replica', 'fsdp'), may hold values from -6 to 6
- gate_weight: bfloat16 [256, 28672], P(None, 'fsdp'), may hold values from -0.375 to 0.375
- down_weight: bfloat16 [28672, 256], P('fsdp'), may hold values from -0.03125 to 0.03125
- local_up: bfloat16 [16, 256, 28672], P('replica', None, 'fsdp'), may hold values from -6 to 6
- deltas: bfloat16 [16, 256, 28672], P('replica', None, 'fsdp'), may hold values from -6 to 6
- outer_up: float32 [256, 28672], P('replica', 'fsdp'), may hold values from -6 to 6
- momentum: float32 [256, 28672], P('replica', 'fsdp'), may hold values from -3 to 3
Outputs:
- inner_out: bfloat16 [16, 4096, 256], P('replica', 'fsdp')
- merged_up: bfloat16 [16, 256, 28672], P('replica', None, 'fsdp')
- new_outer: float32 [256, 28672], P('replica', 'fsdp')
- new_momentum: float32 [256, 28672], P('replica', 'fsdp')
The draws below stay inside these ranges and needn't reach their ends.
All inputs are finite; a program needn't handle non-finite values.
Results may differ from the reference program's by a relative error of at most 0.02.
Values may be sent and summed in bfloat16 or wider, within the bound.
A program may use at most 64 MiB of HBM per device.

```python
import jax
import jax.numpy as jnp
from jax import lax

FF = 28672
ROWS = 256
GROUP_TOK = 4096
N_REPLICA = 16
N_FSDP = 32


def steps_of(stream_key, dims, shards, low, largest):
    def one(position, shards_of):
        draws = jax.random.uniform(jax.random.fold_in(jax.random.fold_in(stream_key, 6), position), (shards_of,), jnp.float32, low / len(shards), largest / len(shards))
        return jnp.repeat(jnp.exp(draws), dims[position] // shards_of).reshape((-1,) + (1,) * (len(dims) - position - 1))

    level = one(*shards[0])
    for cut in shards[1:]:
        level = level * one(*cut)
    return level


def gaussian(own_key, dims, deviation, limit, shards=(), kind=jnp.bfloat16):
    array = jax.random.normal(own_key, dims, jnp.float32) * deviation
    if len(shards) > 0:
        array = steps_of(own_key, dims, shards, -0.22, 0.18) * array
    return jnp.clip(array, min=-limit, max=limit).astype(kind)


def setup_inputs(seed: int = 0) -> dict:
    key_list = jax.random.split(jax.random.key(seed), 8)
    return {
        "tokens": gaussian(key_list[0], (N_REPLICA, GROUP_TOK, ROWS), 1.0, 6.0, ((0, 16), (1, 32))),
        "gate_weight": gaussian(key_list[1], (ROWS, FF), ROWS ** -0.5, 0.375, ((1, 32),)),
        "down_weight": gaussian(key_list[2], (FF, ROWS), FF ** -0.5, 0.03125, ((0, 32),)),
        "local_up": gaussian(key_list[3], (N_REPLICA, ROWS, FF), 1.0, 6.0, ((0, 16), (2, 32))),
        "deltas": gaussian(key_list[4], (N_REPLICA, ROWS, FF), 1.0, 6.0, ((0, 16), (2, 32))),
        "outer_up": gaussian(key_list[5], (ROWS, FF), 1.0, 6.0, ((0, 16), (1, 32)), jnp.float32),
        "momentum": gaussian(key_list[6], (ROWS, FF), 0.5, 3.0, ((0, 16), (1, 32)), jnp.float32),
    }


outer_rate = 0.7
momentum_coef = 0.9
mix_weight = 0.5


def reference(tokens, gate_weight, down_weight, local_up, deltas, outer_up, momentum):
    block_width = FF // N_FSDP
    down_blocks = down_weight.reshape(N_FSDP, block_width, ROWS)

    def forward(pair):
        rows, up_slab = pair
        gate = jnp.dot(rows, gate_weight, preferred_element_type=jnp.float32)
        upper = jnp.dot(rows, up_slab, preferred_element_type=jnp.float32) * (ROWS ** -0.5)
        hidden = (jax.nn.silu(gate) * upper).astype(jnp.bfloat16)
        hidden_blocks = jnp.transpose(hidden.reshape(hidden.shape[0], N_FSDP, block_width), (1, 0, 2))

        def one_block(carry, blocks):
            left, right = blocks
            partial_value = jnp.dot(left, right, preferred_element_type=jnp.float32).astype(jnp.bfloat16)
            partial_value = lax.optimization_barrier(partial_value).astype(jnp.float32)
            return carry + partial_value, None

        start = jnp.zeros((hidden.shape[0], ROWS), jnp.float32)
        summed, unused = lax.scan(one_block, start, (hidden_blocks, down_blocks))
        return summed.astype(jnp.bfloat16)

    inner_out = lax.map(forward, (tokens, local_up))
    total = jnp.sum(deltas.astype(jnp.float32), axis=0)
    grad = total / N_REPLICA
    new_momentum = momentum_coef * momentum + grad
    new_outer = outer_up - outer_rate * (grad + momentum_coef * new_momentum)
    outer_half = lax.optimization_barrier(new_outer.astype(jnp.bfloat16)).astype(jnp.float32)
    merged_up = (mix_weight * local_up.astype(jnp.float32) + (1.0 - mix_weight) * outer_half[None]).astype(jnp.bfloat16)
    return inner_out, merged_up, new_outer, new_momentum
```

```python
import jax
import jax.numpy as jnp
from jax import lax
from jax.experimental import pallas as pl
from jax.experimental.pallas import tpu as pltpu
from jax.sharding import PartitionSpec as P

MESH = pl.DeviceIdType.MESH
BF16, F32 = jnp.bfloat16, jnp.float32

NX, NYLO, NZ = 4, 4, 8
N_REPLICA = NX * NYLO
ROWS = 256

outer_rate = 0.7
momentum_coef = 0.9
mix_weight = 0.5

OWN, PAR = 0, 1
BASE = ((0, 1, 4, 8, 12), (3, 6, 10, 13, 15))
N_SLOT = 16

GATHER_AT = {
    1: ((OWN, 1),),
    2: ((PAR, 0),),
    3: ((OWN, 2),),
    5: ((PAR, 1),),
    7: ((OWN, 3),),
    9: ((PAR, 2),),
    11: ((OWN, 4),),
    12: ((PAR, 3),),
    14: ((PAR, 4),),
}
REDUCE_AT = {
    11: ((OWN, 1, 3),),
    14: ((OWN, 0, 4),),
    15: ((OWN, 1, 2),),
}
OUTER_AT = {6: 2, 10: 3, 13: 4}


def kernel(
    tokens, gate_w, down_w, local_up, deltas, outer_up, momentum,
    inner_out, merged_up, new_outer, new_momentum,
    tok, gate_v, up_v, down_v, delta_v, outer_v, mom_v,
    part, sib_part, rs_in, rs_out, y_in, own_sum,
    x_in, y_mid, y_sum_in, half_all, merged_v, out_v, no_v, nm_v,
    load_sem, store_sem, ag_send, ag_recv, ag_sib_send, ag_sib_recv,
    ps_send, ps_recv, rs_send, rs_recv, yx_send, yx_recv, o_send, o_recv,
):
    r, f = lax.axis_index("replica"), lax.axis_index("fsdp")
    x, ylo = r // NYLO, r % NYLO
    z, yh, c = f // 4, (f // 2) % 2, f % 2
    a = 1 - 2 * c
    blk = tokens.shape[1]

    def dev(x=x, ylo=ylo, z=z, yh=yh, c=c):
        return (x * NYLO + ylo, z * 4 + yh * 2 + c)

    sibling = dev(c=1 - c)
    partner = dev(yh=1 - yh)
    ahead = (dev(z=(z + a + NZ) % NZ), dev(z=(z - a + NZ) % NZ))
    x_peer = [dev(x=(x + k) % NX) for k in range(1, NX)]
    y_peer = [dev(ylo=(ylo + k) % NYLO) for k in range(1, NYLO)]
    peers = [sibling, partner, *ahead, *x_peer, *y_peer]

    def remote(src, dst, ssem, rsem, to):
        return pltpu.make_async_remote_copy(
            src_ref=src, dst_ref=dst, send_sem=ssem, recv_sem=rsem, device_id=to, device_id_type=MESH
        )

    mine = pl.ds(pl.multiple_of(c * blk, blk), blk)
    other = pl.ds(pl.multiple_of((1 - c) * blk, blk), blk)

    x_rows = ROWS // NX
    y_rows = ROWS // N_REPLICA
    my_x = pl.ds(pl.multiple_of(x * x_rows, x_rows), x_rows)
    loads = [
        pltpu.make_async_copy(tokens.at[0], tok.at[0, mine], load_sem.at[0]),
        pltpu.make_async_copy(gate_w, gate_v, load_sem.at[1]),
        pltpu.make_async_copy(local_up.at[0], up_v, load_sem.at[2]),
        pltpu.make_async_copy(down_w, down_v, load_sem.at[3]),
        pltpu.make_async_copy(deltas.at[0, my_x], delta_v, load_sem.at[4]),
        pltpu.make_async_copy(outer_up, outer_v, load_sem.at[5]),
        pltpu.make_async_copy(momentum, mom_v, load_sem.at[6]),
    ]
    for load in loads:
        load.start()

    barrier = pltpu.get_barrier_semaphore()
    for peer in peers:
        pl.semaphore_signal(barrier, inc=1, device_id=peer, device_id_type=MESH)
    pl.semaphore_wait(barrier, len(peers))

    def slot_from(side, q, j):
        if j in (0, 4):
            return BASE[side][j]
        return BASE[side][j] + (1 - c if q == 0 else c)

    def slot_to(side, q, j):
        if j in (0, 4):
            return BASE[side][j]
        return BASE[side][j] + (c if q == 0 else 1 - c)

    def pass_on(side, q, j, src):
        s = slot_from(side, q, j + 1)
        return remote(src, tok.at[s, mine], ag_send.at[s], ag_recv.at[s], ahead[q])

    def to_sibling(s, src):
        return remote(src, tok.at[s, mine], ag_sib_send.at[s], ag_sib_recv.at[s], sibling)

    def y_tokens():
        s = BASE[PAR][0]
        return remote(tokens.at[0], tok.at[s, mine], yx_send.at[0], ag_recv.at[s], partner)

    def gathered(side, j):
        if j == 0:
            s = BASE[side][0]
            y_tokens().wait_recv()
            src = tok.at[s, mine]
            for q in (0, 1):
                pass_on(side, q, 0, src).start()
            to_sibling(s, src).start()
            return
        for q in (0, 1) if j < 4 else (0,):
            s = slot_from(side, q, j)
            src = tok.at[s, mine]
            remote(src, src, ag_send.at[s], ag_recv.at[s], ahead[q]).wait_recv()
            if j < (4 if q == 0 else 3):
                pass_on(side, q, j, src).start()
            to_sibling(s, src).start()

    def rs_index(side, q, j):
        return side * 7 + (4 - j if q == 0 else 4 + 3 - j)

    def rs_copy(side, q, j):
        i = rs_index(side, q, j)
        return remote(rs_out.at[i], rs_in.at[i], rs_send.at[i], rs_recv.at[i], ahead[q])

    def sib_copy(s):
        return remote(part.at[s, other], sib_part.at[s], ps_send.at[s], ps_recv.at[s], sibling)

    def my_terms(s):
        sib_copy(s).wait_recv()
        return part[s, mine, :].astype(F32) + sib_part[s].astype(F32)

    def reduce_send(side, q, j):
        total = my_terms(slot_to(side, q, j))
        if j < (4 if q == 0 else 3):
            before = rs_copy(side, q, j + 1)
            before.wait_recv()
            total = total + rs_in[rs_index(side, q, j + 1)].astype(F32)
        rs_out[rs_index(side, q, j)] = total.astype(BF16)
        rs_copy(side, q, j).start()

    def reduce_last(side):
        total = my_terms(BASE[side][0])
        for q in (0, 1):
            rs_copy(side, q, 1).wait_recv()
            total = total + rs_in[rs_index(side, q, 1)].astype(F32)
        return total

    def rows_of(k):
        return pl.ds(pl.multiple_of(k * y_rows, y_rows), y_rows)

    def x_leg(k):
        px = (x + k + 1) % NX
        rows = pl.ds(pl.multiple_of(px * x_rows, x_rows), x_rows)
        return remote(deltas.at[0, rows], x_in.at[k], o_send.at[k], o_recv.at[k], x_peer[k])

    def y_leg(k):
        py = (ylo + k + 1) % NYLO
        return remote(y_mid.at[rows_of(py)], y_sum_in.at[k], o_send.at[3 + k], o_recv.at[3 + k], y_peer[k])

    def y_gather(k):
        rows = rows_of(r)
        return remote(half_all.at[rows], half_all.at[rows], o_send.at[6 + k], o_recv.at[6 + k], y_peer[k])

    def x_gather(k):
        return remote(half_all.at[my_x], half_all.at[my_x], o_send.at[9 + k], o_recv.at[9 + k], x_peer[k])

    stores = [
        pltpu.make_async_copy(no_v, new_outer, store_sem.at[0]),
        pltpu.make_async_copy(nm_v, new_momentum, store_sem.at[1]),
        pltpu.make_async_copy(merged_v, merged_up.at[0], store_sem.at[2]),
        pltpu.make_async_copy(out_v, inner_out.at[0], store_sem.at[3]),
    ]

    def outer(stage):
        if stage == 1:
            for k in range(3):
                x_leg(k).start()
        elif stage == 2:
            loads[4].wait()
            total = delta_v[...].astype(F32)
            for k in range(3):
                x_leg(k).wait_recv()
                total = total + x_in[k].astype(F32)
            y_mid[...] = total.astype(BF16)
            for k in range(3):
                y_leg(k).start()
        elif stage == 3:
            loads[5].wait()
            loads[6].wait()
            total = y_mid[rows_of(ylo), :].astype(F32)
            for k in range(3):
                y_leg(k).wait_recv()
                total = total + y_sum_in[k].astype(F32)
            grad = total / N_REPLICA
            nm = momentum_coef * mom_v[...] + grad
            no = outer_v[...] - outer_rate * (grad + momentum_coef * nm)
            nm_v[...] = nm
            no_v[...] = no
            half_all[rows_of(r), :] = no.astype(BF16)
            for k in range(3):
                y_gather(k).start()
            stores[0].start()
            stores[1].start()
        elif stage == 4:
            for k in range(3):
                y_gather(k).wait_recv()
            for k in range(3):
                x_gather(k).start()
        else:
            for k in range(3):
                x_gather(k).wait_recv()
            merged = mix_weight * up_v[...].astype(F32) + (1.0 - mix_weight) * half_all[...].astype(F32)
            merged_v[...] = merged.astype(BF16)
            stores[2].start()

    for q in (0, 1):
        pass_on(OWN, q, 0, tokens.at[0]).start()
    y_tokens().start()
    to_sibling(0, tokens.at[0]).start()
    outer(1)
    for load in loads[:4]:
        load.wait()

    def compute(s):
        rows = tok[s]
        total = jnp.zeros((rows.shape[0], down_v.shape[1]), F32)
        width = gate_v.shape[1]
        for start in range(0, width, 256):
            cols = slice(start, min(start + 256, width))
            gate = jnp.dot(rows, gate_v[:, cols], preferred_element_type=F32)
            upper = jnp.dot(rows, up_v[:, cols], preferred_element_type=F32)
            hidden = ((gate + gate * jnp.tanh(0.5 * gate)) * upper).astype(BF16)
            total = total + jnp.dot(hidden, down_v[cols, :], preferred_element_type=F32)
        part[s] = (total * (0.5 * ROWS ** -0.5)).astype(BF16)

    def step(s, carry):
        for at in range(N_SLOT):
            if at in GATHER_AT or at in REDUCE_AT or at in OUTER_AT:

                @pl.when(s == at)
                def _():
                    for side, j in GATHER_AT.get(at, ()):
                        gathered(side, j)
                    for side, q, j in REDUCE_AT.get(at, ()):
                        reduce_send(side, q, j)
                    if at in OUTER_AT:
                        outer(OUTER_AT[at])

        half = tok.at[s, other]
        remote(half, half, ag_sib_send.at[s], ag_sib_recv.at[s], sibling).wait_recv()
        compute(s)
        sib_copy(s).start()
        return carry

    lax.fori_loop(0, N_SLOT, step, 0)

    reduce_send(PAR, 1, 3)
    reduce_send(PAR, 0, 4)
    reduce_send(OWN, 0, 3)
    reduce_send(OWN, 1, 1)
    reduce_send(PAR, 1, 2)
    reduce_send(PAR, 0, 3)
    reduce_send(OWN, 0, 2)
    reduce_send(PAR, 1, 1)
    reduce_send(PAR, 0, 2)
    reduce_send(OWN, 0, 1)
    outer(5)
    reduce_send(PAR, 0, 1)
    y_final = remote(rs_out.at[14], y_in, yx_send.at[1], yx_recv.at[0], partner)
    rs_out[14] = reduce_last(PAR).astype(BF16)
    y_final.start()
    own_sum[...] = reduce_last(OWN)
    y_final.wait_recv()
    out_v[...] = (own_sum[...] + y_in[...].astype(F32)).astype(BF16)
    stores[3].start()

    for side in (OWN, PAR):
        for j in range(0, 4):
            for q in (0, 1):
                if j < (4 if q == 0 else 3):
                    pass_on(side, q, j, tok.at[0, mine]).wait_send()
    y_tokens().wait_send()
    y_final.wait_send()
    for s in range(N_SLOT):
        to_sibling(s, tok.at[s, mine]).wait_send()
        sib_copy(s).wait_send()
    for side in (OWN, PAR):
        for j in range(1, 5):
            for q in (0, 1):
                if j < 4 or q == 0:
                    rs_copy(side, q, j).wait_send()
    for k in range(3):
        x_leg(k).wait_send()
        y_leg(k).wait_send()
        y_gather(k).wait_send()
        x_gather(k).wait_send()
    for store in stores:
        store.wait()


def body(tokens, gate_weight, down_weight, local_up, deltas, outer_up, momentum):
    blk, rows = tokens.shape[1:]
    width = gate_weight.shape[1]
    share = outer_up.shape[0]
    dma = pltpu.SemaphoreType.DMA
    return pl.pallas_call(
        kernel,
        out_shape=(
            jax.ShapeDtypeStruct(tokens.shape, BF16),
            jax.ShapeDtypeStruct(local_up.shape, BF16),
            jax.ShapeDtypeStruct(outer_up.shape, F32),
            jax.ShapeDtypeStruct(momentum.shape, F32),
        ),
        in_specs=[pl.BlockSpec(memory_space=pl.ANY)] * 7,
        out_specs=[pl.BlockSpec(memory_space=pl.ANY)] * 4,
        scratch_shapes=[
            pltpu.VMEM((N_SLOT, 2 * blk, rows), BF16),
            pltpu.VMEM(gate_weight.shape, BF16),
            pltpu.VMEM(local_up.shape[1:], BF16),
            pltpu.VMEM(down_weight.shape, BF16),
            pltpu.VMEM((ROWS // NX, width), BF16),
            pltpu.VMEM((share, width), F32),
            pltpu.VMEM((share, width), F32),
            pltpu.VMEM((N_SLOT, 2 * blk, rows), BF16),
            pltpu.VMEM((N_SLOT, blk, rows), BF16),
            pltpu.VMEM((14, blk, rows), BF16),
            pltpu.VMEM((15, blk, rows), BF16),
            pltpu.VMEM((blk, rows), BF16),
            pltpu.VMEM((blk, rows), F32),
            pltpu.VMEM((NX - 1, ROWS // NX, width), BF16),
            pltpu.VMEM((ROWS // NX, width), BF16),
            pltpu.VMEM((NYLO - 1, share, width), BF16),
            pltpu.VMEM((ROWS, width), BF16),
            pltpu.VMEM((ROWS, width), BF16),
            pltpu.VMEM((blk, rows), BF16),
            pltpu.VMEM((share, width), F32),
            pltpu.VMEM((share, width), F32),
            dma((7,)),
            dma((4,)),
            dma((N_SLOT,)),
            dma((N_SLOT,)),
            dma((N_SLOT,)),
            dma((N_SLOT,)),
            dma((N_SLOT,)),
            dma((N_SLOT,)),
            dma((14,)),
            dma((14,)),
            dma((2,)),
            dma((1,)),
            dma((12,)),
            dma((12,)),
        ],
        compiler_params=pltpu.CompilerParams(
            collective_id=0, has_side_effects=True, vmem_limit_bytes=48 * 1024 * 1024
        ),
        cost_estimate=pl.CostEstimate(flops=5_700_000_000, bytes_accessed=3_000_000, transcendentals=3_700_000),
    )(tokens, gate_weight, down_weight, local_up, deltas, outer_up, momentum)


def solution(mesh):
    placed = (
        P("replica", "fsdp", None),
        P(None, "fsdp"),
        P("fsdp", None),
        P("replica", None, "fsdp"),
        P("replica", None, "fsdp"),
        P("replica", "fsdp"),
        P("replica", "fsdp"),
    )
    return jax.shard_map(
        body,
        mesh=mesh,
        in_specs=placed,
        out_specs=(
            P("replica", "fsdp", None),
            P("replica", None, "fsdp"),
            P("replica", "fsdp"),
            P("replica", "fsdp"),
        ),
        check_vma=False,
    )
```

```python
import jax
import jax.numpy as jnp
from jax import lax
from jax.experimental import pallas as pl
from jax.experimental.pallas import tpu as pltpu
from jax.sharding import PartitionSpec as P

MESH = pl.DeviceIdType.MESH
BF16, F32 = jnp.bfloat16, jnp.float32

NX, NYLO, NZ = 4, 4, 8
N_REPLICA = NX * NYLO
ROWS = 256

outer_rate = 0.7
momentum_coef = 0.9
mix_weight = 0.5

OWN, PAR = 0, 1
TREE = (
    ({1: 0, 2: 1, 3: 1, 4: 2}, {1: 0, 2: 1, 3: 2}),
    ({1: 0, 2: 0, 3: 2, 4: 2}, {1: 0, 2: 0, 3: 2}),
)
PAIRS = (
    ((0, 0, 0), (0, 0, 1)),
    ((0, 1, 1), (1, 0, 0)),
    ((0, 0, 2), (0, 1, 2)),
    ((1, 0, 1), (1, 0, 2)),
    ((1, 1, 1), (1, 1, 2)),
    ((0, 0, 3), (0, 1, 3)),
    ((1, 0, 4), (1, 0, 3)),
    ((0, 0, 4), (1, 1, 3)),
)
SLOT = {block: 2 * i + k for i, pair in enumerate(PAIRS) for k, block in enumerate(pair)}
N_SLOT = len(SLOT)

BEFORE = (
    (("g", 0, 0, 1),),
    (("g", 0, 1, 1),),
    (("y",),),
    (("g", 0, 0, 2),),
    (("g", 0, 0, 3), ("g", 0, 1, 2), ("o", 2)),
    (("g", 1, 0, 1),),
    (("g", 1, 0, 2),),
    (("g", 1, 1, 1),),
    (("r", 1, 0, 1), ("g", 1, 1, 2)),
    (),
    (("g", 0, 0, 4), ("r", 1, 1, 1), ("g", 0, 1, 3)),
    (("g", 1, 0, 3), ("o", 3)),
    (("r", 0, 0, 3), ("g", 1, 0, 4), ("r", 0, 1, 3)),
    (),
    (("g", 1, 1, 3), ("r", 1, 0, 4), ("r", 1, 0, 3)),
    (),
)
AFTER = (
    ("r", 1, 1, 3), ("r", 0, 0, 4), ("r", 0, 1, 2), ("o", 4), ("w", 0), ("r", 1, 0, 2), ("r", 1, 1, 2),
    ("r", 0, 0, 2), ("r", 0, 1, 1), ("w", 1), ("f", 1), ("r", 0, 0, 1), ("o", 5), ("w", 2), ("f", 0),
)


def kernel(
    tokens, gate_w, down_w, local_up, deltas, outer_up, momentum,
    out_v, merged_v, no_v, nm_v,
    tok, gate_v, up_v, down_v, delta_v, outer_v, mom_v,
    part, acc, rs_in, rs_out, y_out, y_in,
    x_in, y_mid, y_sum_in, half_all,
    load_sem, w_send, w_recv, ag_send, ag_recv, rs_send, rs_recv, y_send, y_recv, o_send, o_recv,
):
    r, f = lax.axis_index("replica"), lax.axis_index("fsdp")
    x, ylo = r // NYLO, r % NYLO
    z, yh, c = f // 4, (f // 2) % 2, f % 2
    a = 1 - 2 * c

    def dev(x=x, ylo=ylo, z=z, yh=yh, c=c):
        return (x * NYLO + ylo, z * 4 + yh * 2 + c)

    def along(q, d):
        return dev(z=(z + (a if q == 0 else -a) * d + NZ) % NZ)

    sibling = dev(c=1 - c)
    partner = dev(yh=1 - yh)
    x_peer = [dev(x=(x + k) % NX) for k in range(1, NX)]
    y_peer = [dev(ylo=(ylo + k) % NYLO) for k in range(1, NYLO)]
    steps = sorted({j - p for side in TREE for edges in side for j, p in edges.items()})
    peers = [sibling, partner, *x_peer, *y_peer] + [along(q, d) for d in steps for q in (0, 1)]

    def remote(src, dst, ssem, rsem, to):
        return pltpu.make_async_remote_copy(
            src_ref=src, dst_ref=dst, send_sem=ssem, recv_sem=rsem, device_id=to, device_id_type=MESH
        )

    x_rows = ROWS // NX
    y_rows = ROWS // N_REPLICA
    my_x = pl.ds(pl.multiple_of(x * x_rows, x_rows), x_rows)
    loads = [
        pltpu.make_async_copy(tokens.at[0], tok.at[SLOT[0, 0, 0]], load_sem.at[0]),
        pltpu.make_async_copy(gate_w, gate_v.at[0], load_sem.at[1]),
        pltpu.make_async_copy(local_up.at[0], up_v.at[0], load_sem.at[2]),
        pltpu.make_async_copy(down_w, down_v.at[0], load_sem.at[3]),
        pltpu.make_async_copy(deltas.at[0, my_x], delta_v, load_sem.at[4]),
        pltpu.make_async_copy(outer_up, outer_v, load_sem.at[5]),
        pltpu.make_async_copy(momentum, mom_v, load_sem.at[6]),
    ]
    for load in loads:
        load.start()

    barrier = pltpu.get_barrier_semaphore()
    for peer in peers:
        pl.semaphore_signal(barrier, inc=1, device_id=peer, device_id_type=MESH)
    pl.semaphore_wait(barrier, len(peers))

    def slot(side, q, j):
        return SLOT[side, 0 if j == 0 else q, j]

    def children(side, q, p):
        return [j for j, parent in TREE[side][q].items() if parent == p]

    def gather_copy(side, q, j, src=None):
        p, s = TREE[side][q][j], slot(side, q, j)
        src = tok.at[slot(side, q, p)] if src is None else src
        return remote(src, tok.at[s], ag_send.at[s], ag_recv.at[s], along(q, j - p))

    def y_tokens():
        s = SLOT[PAR, 0, 0]
        return remote(tokens.at[0], tok.at[s], y_send.at[0], ag_recv.at[s], partner)

    def reduce_copy(side, q, j):
        p, s = TREE[side][q][j], slot(side, q, j)
        src = rs_out if children(side, q, j) else part
        return remote(src.at[s], rs_in.at[s], rs_send.at[s], rs_recv.at[s], along(q, p - j))

    def sum_of(side, j, dirs):
        total = part[slot(side, dirs[0], j)].astype(F32)
        for q in dirs:
            for child in children(side, q, j):
                reduce_copy(side, q, child).wait_recv()
                total = total + rs_in[slot(side, q, child)].astype(F32)
        return total

    y_final = remote(y_out, y_in, y_send.at[1], y_recv.at[0], partner)

    def rows_of(k):
        return pl.ds(pl.multiple_of(k * y_rows, y_rows), y_rows)

    def x_leg(k):
        px = (x + k + 1) % NX
        rows = pl.ds(pl.multiple_of(px * x_rows, x_rows), x_rows)
        return remote(deltas.at[0, rows], x_in.at[k], o_send.at[k], o_recv.at[k], x_peer[k])

    def y_leg(k):
        py = (ylo + k + 1) % NYLO
        return remote(y_mid.at[rows_of(py)], y_sum_in.at[k], o_send.at[3 + k], o_recv.at[3 + k], y_peer[k])

    def y_gather(k):
        rows = rows_of(r)
        return remote(half_all.at[rows], half_all.at[rows], o_send.at[6 + k], o_recv.at[6 + k], y_peer[k])

    def x_gather(k):
        return remote(half_all.at[my_x], half_all.at[my_x], o_send.at[9 + k], o_recv.at[9 + k], x_peer[k])

    def outer(stage):
        if stage == 2:
            loads[4].wait()
            total = delta_v[...].astype(F32)
            for k in range(3):
                x_leg(k).wait_recv()
                total = total + x_in[k].astype(F32)
            y_mid[...] = total.astype(BF16)
            for k in range(3):
                y_leg(k).start()
        elif stage == 3:
            loads[5].wait()
            loads[6].wait()
            total = y_mid[rows_of(ylo), :].astype(F32)
            for k in range(3):
                y_leg(k).wait_recv()
                total = total + y_sum_in[k].astype(F32)
            grad = total / N_REPLICA
            nm = momentum_coef * mom_v[...] + grad
            no = outer_v[...] - outer_rate * (grad + momentum_coef * nm)
            nm_v[...] = nm
            no_v[...] = no
            half_all[rows_of(r), :] = no.astype(BF16)
            for k in range(3):
                y_gather(k).start()
        elif stage == 4:
            for k in range(3):
                y_gather(k).wait_recv()
            for k in range(3):
                x_gather(k).start()
        else:
            for k in range(3):
                x_gather(k).wait_recv()
            merged = mix_weight * up_v[0].astype(F32) + (1.0 - mix_weight) * half_all[...].astype(F32)
            merged_v[...] = merged.astype(BF16)

    weights = [
        remote(src, dst.at[1], w_send.at[k], w_recv.at[k], sibling)
        for k, (src, dst) in enumerate(((gate_w, gate_v), (local_up.at[0], up_v), (down_w, down_v)))
    ]

    def wait_sends(stage):
        if stage == 0:
            for weight in weights:
                weight.wait_send()
            y_tokens().wait_send()
            for side in (OWN, PAR):
                for q in (0, 1):
                    for j in TREE[side][q]:
                        gather_copy(side, q, j).wait_send()
            for k in range(3):
                x_leg(k).wait_send()
                y_leg(k).wait_send()
        elif stage == 1:
            for k in range(3):
                y_gather(k).wait_send()
        else:
            for k in range(3):
                x_gather(k).wait_send()
            for side in (OWN, PAR):
                for q in (0, 1):
                    for j in TREE[side][q]:
                        reduce_copy(side, q, j).wait_send()
            y_final.wait_send()

    def act(kind, *what):
        if kind == "g":
            side, q, j = what
            s = slot(side, q, j)
            gather_copy(side, q, j).wait_recv()
            for child in children(side, q, j):
                gather_copy(side, q, child).start()
        elif kind == "y":
            y_tokens().wait_recv()
            for q in (0, 1):
                for child in children(PAR, q, 0):
                    gather_copy(PAR, q, child).start()
        elif kind == "r":
            side, q, j = what
            if children(side, q, j):
                rs_out[slot(side, q, j)] = sum_of(side, j, (q,)).astype(BF16)
            reduce_copy(side, q, j).start()
        elif kind == "f":
            total = sum_of(what[0], 0, (0, 1))
            if what[0] == PAR:
                y_out[...] = total.astype(BF16)
                y_final.start()
            else:
                y_final.wait_recv()
                out_v[...] = (total + y_in[...].astype(F32)).astype(BF16)
        elif kind == "o":
            outer(what[0])
        else:
            wait_sends(what[0])

    for q in (0, 1):
        for child in children(OWN, q, 0):
            gather_copy(OWN, q, child, tokens.at[0]).start()
    y_tokens().start()
    for weight in weights:
        weight.start()
    for k in range(3):
        x_leg(k).start()
    for load in loads[:4]:
        load.wait()

    blk, width = tok.shape[1], gate_v.shape[2]

    def compute(i, h):
        rows = tok[pl.ds(2 * i, 2)].reshape(2 * blk, ROWS)
        total = jnp.zeros((2 * blk, ROWS), F32)
        for start in range(0, width, 256):
            cols = slice(start, min(start + 256, width))
            gate = jnp.dot(rows, gate_v[h, :, cols], preferred_element_type=F32)
            upper = jnp.dot(rows, up_v[h, :, cols], preferred_element_type=F32)
            hidden = ((gate + gate * jnp.tanh(0.5 * gate)) * upper).astype(BF16)
            total = total + jnp.dot(hidden, down_v[h, cols, :], preferred_element_type=F32)

        @pl.when(h == 0)
        def _():
            acc[...] = total

        @pl.when(h == 1)
        def _():
            both = (acc[...] + total) * (0.5 * ROWS ** -0.5)
            part[pl.ds(2 * i, 2)] = both.astype(BF16).reshape(2, blk, ROWS)

    def unit(u, carry):
        for at, todo in enumerate(BEFORE):
            if todo or at == 1:

                @pl.when(u == at)
                def _():
                    for what in todo:
                        act(*what)
                    if at == 1:
                        for weight in weights:
                            weight.wait_recv()

        compute(u // 2, u % 2)
        return carry

    lax.fori_loop(0, len(BEFORE), unit, 0)
    for what in AFTER:
        act(*what)


def store_kernel(*refs):
    n = (len(refs) - 1) // 2
    copies = [pltpu.make_async_copy(src, dst, refs[-1].at[k]) for k, (src, dst) in enumerate(zip(refs[:n], refs[n:-1]))]
    for copy in copies:
        copy.start()
    for copy in copies:
        copy.wait()


def body(tokens, gate_weight, down_weight, local_up, deltas, outer_up, momentum):
    blk, rows = tokens.shape[1:]
    width = gate_weight.shape[1]
    share = outer_up.shape[0]
    dma = pltpu.SemaphoreType.DMA
    outs = (
        ((blk, rows), BF16, tokens.shape),
        ((ROWS, width), BF16, local_up.shape),
        ((share, width), F32, outer_up.shape),
        ((share, width), F32, momentum.shape),
    )
    args = [
        pltpu.with_memory_space_constraint(arg, pltpu.HBM)
        for arg in (tokens, gate_weight, down_weight, local_up, deltas, outer_up, momentum)
    ]
    held = pl.pallas_call(
        kernel,
        out_shape=tuple(pltpu.VMEM(shape, kind) for shape, kind, _ in outs),
        in_specs=[pl.BlockSpec(memory_space=pltpu.HBM)] * 7,
        out_specs=[pl.BlockSpec(memory_space=pltpu.VMEM)] * 4,
        scratch_shapes=[
            pltpu.VMEM((N_SLOT, blk, rows), BF16),
            pltpu.VMEM((2, ROWS, width), BF16),
            pltpu.VMEM((2, ROWS, width), BF16),
            pltpu.VMEM((2, width, ROWS), BF16),
            pltpu.VMEM((ROWS // NX, width), BF16),
            pltpu.VMEM((share, width), F32),
            pltpu.VMEM((share, width), F32),
            pltpu.VMEM((N_SLOT, blk, rows), BF16),
            pltpu.VMEM((2 * blk, rows), F32),
            pltpu.VMEM((N_SLOT, blk, rows), BF16),
            pltpu.VMEM((N_SLOT, blk, rows), BF16),
            pltpu.VMEM((blk, rows), BF16),
            pltpu.VMEM((blk, rows), BF16),
            pltpu.VMEM((NX - 1, ROWS // NX, width), BF16),
            pltpu.VMEM((ROWS // NX, width), BF16),
            pltpu.VMEM((NYLO - 1, share, width), BF16),
            pltpu.VMEM((ROWS, width), BF16),
            dma((7,)),
            dma((3,)),
            dma((3,)),
            dma((N_SLOT,)),
            dma((N_SLOT,)),
            dma((N_SLOT,)),
            dma((N_SLOT,)),
            dma((2,)),
            dma((1,)),
            dma((12,)),
            dma((12,)),
        ],
        compiler_params=pltpu.CompilerParams(
            collective_id=0, has_side_effects=True, vmem_limit_bytes=32 * 1024 * 1024
        ),
        cost_estimate=pl.CostEstimate(flops=5_700_000_000, bytes_accessed=3_000_000, transcendentals=3_700_000),
    )(*args)
    inner_out, merged_up, new_outer, new_momentum = pl.pallas_call(
        store_kernel,
        out_shape=tuple(jax.ShapeDtypeStruct(shape, kind) for shape, kind, _ in outs),
        in_specs=[pl.BlockSpec(memory_space=pltpu.VMEM)] * 4,
        out_specs=[pl.BlockSpec(memory_space=pl.ANY)] * 4,
        scratch_shapes=[dma((4,))],
    )(*held)
    return inner_out[None], merged_up[None], new_outer, new_momentum


def solution(mesh):
    placed = (
        P("replica", "fsdp", None),
        P(None, "fsdp"),
        P("fsdp", None),
        P("replica", None, "fsdp"),
        P("replica", None, "fsdp"),
        P("replica", "fsdp"),
        P("replica", "fsdp"),
    )
    return jax.shard_map(
        body,
        mesh=mesh,
        in_specs=placed,
        out_specs=(
            P("replica", "fsdp", None),
            P("replica", None, "fsdp"),
            P("replica", "fsdp"),
            P("replica", "fsdp"),
        ),
        check_vma=False,
    )
```

```python
import jax
import jax.numpy as jnp
from jax import lax
from jax.experimental import pallas as pl
from jax.experimental.pallas import tpu as pltpu
from jax.sharding import PartitionSpec as P

MESH = pl.DeviceIdType.MESH
BF16, F32 = jnp.bfloat16, jnp.float32

NX, NYLO, NZ = 4, 4, 8
N_REPLICA = NX * NYLO
ROWS = 256

outer_rate = 0.7
momentum_coef = 0.9
mix_weight = 0.5

OWN, PAR = 0, 1
TREE = (
    ({1: 0, 2: 1, 3: 1, 4: 2}, {1: 0, 2: 1, 3: 2}),
    ({1: 0, 2: 0, 3: 2, 4: 2}, {1: 0, 2: 0, 3: 2}),
)
PAIRS = (
    ((0, 0, 0), (0, 0, 1)),
    ((0, 1, 1), (1, 0, 0)),
    ((0, 0, 2), (0, 1, 2)),
    ((1, 0, 1), (1, 0, 2)),
    ((1, 1, 1), (1, 1, 2)),
    ((0, 0, 3), (0, 1, 3)),
    ((1, 0, 4), (1, 0, 3)),
    ((0, 0, 4), (1, 1, 3)),
)
SLOT = {block: 2 * i + k for i, pair in enumerate(PAIRS) for k, block in enumerate(pair)}
N_SLOT = len(SLOT)

BEFORE = (
    (("g", 0, 0, 1),),
    (("g", 0, 1, 1),),
    (("y",),),
    (("g", 0, 0, 2),),
    (("g", 0, 0, 3), ("g", 0, 1, 2), ("o", 2)),
    (("g", 1, 0, 1),),
    (("g", 1, 0, 2),),
    (("g", 1, 1, 1),),
    (("r", 1, 0, 1), ("g", 1, 1, 2)),
    (),
    (("g", 0, 0, 4), ("r", 1, 1, 1), ("g", 0, 1, 3)),
    (("g", 1, 0, 3), ("o", 3)),
    (("r", 0, 0, 3), ("g", 1, 0, 4), ("r", 0, 1, 3)),
    (),
    (("g", 1, 1, 3), ("r", 1, 0, 4), ("r", 1, 0, 3)),
    (),
)
AFTER = (
    ("r", 1, 1, 3), ("r", 0, 0, 4), ("r", 0, 1, 2), ("o", 4), ("w", 0), ("r", 1, 0, 2), ("r", 1, 1, 2),
    ("r", 0, 0, 2), ("r", 0, 1, 1), ("w", 1), ("f", 1), ("r", 0, 0, 1), ("o", 5), ("w", 2), ("f", 0),
)


def kernel(
    tokens, gate_w, down_w, local_up, deltas, outer_up, momentum,
    out_v, merged_v, no_v, nm_v,
    tok, gate_v, up_v, down_v, delta_v, outer_v, mom_v,
    part, acc, rs_in, rs_out, y_out, y_in,
    x_in, y_mid, y_sum_in, half_all,
    load_sem, w_send, w_recv, ag_send, ag_recv, rs_send, rs_recv, y_send, y_recv, o_send, o_recv,
):
    r, f = lax.axis_index("replica"), lax.axis_index("fsdp")
    x, ylo = r // NYLO, r % NYLO
    z, yh, c = f // 4, (f // 2) % 2, f % 2
    a = 1 - 2 * c

    def dev(x=x, ylo=ylo, z=z, yh=yh, c=c):
        return (x * NYLO + ylo, z * 4 + yh * 2 + c)

    def along(q, d):
        return dev(z=(z + (a if q == 0 else -a) * d + NZ) % NZ)

    sibling = dev(c=1 - c)
    partner = dev(yh=1 - yh)
    x_peer = [dev(x=(x + k) % NX) for k in range(1, NX)]
    y_peer = [dev(ylo=(ylo + k) % NYLO) for k in range(1, NYLO)]
    steps = sorted({j - p for side in TREE for edges in side for j, p in edges.items()})
    peers = [sibling, partner, *x_peer, *y_peer] + [along(q, d) for d in steps for q in (0, 1)]

    def remote(src, dst, ssem, rsem, to):
        return pltpu.make_async_remote_copy(
            src_ref=src, dst_ref=dst, send_sem=ssem, recv_sem=rsem, device_id=to, device_id_type=MESH
        )

    x_rows = ROWS // NX
    y_rows = ROWS // N_REPLICA
    my_x = pl.ds(pl.multiple_of(x * x_rows, x_rows), x_rows)
    loads = [
        pltpu.make_async_copy(tokens.at[0], tok.at[SLOT[0, 0, 0]], load_sem.at[0]),
        pltpu.make_async_copy(gate_w, gate_v.at[0], load_sem.at[1]),
        pltpu.make_async_copy(local_up.at[0], up_v.at[0], load_sem.at[2]),
        pltpu.make_async_copy(down_w, down_v.at[0], load_sem.at[3]),
        pltpu.make_async_copy(deltas.at[0, my_x], delta_v, load_sem.at[4]),
        pltpu.make_async_copy(outer_up, outer_v, load_sem.at[5]),
        pltpu.make_async_copy(momentum, mom_v, load_sem.at[6]),
    ]
    for load in loads:
        load.start()

    barrier = pltpu.get_barrier_semaphore()
    for peer in peers:
        pl.semaphore_signal(barrier, inc=1, device_id=peer, device_id_type=MESH)
    pl.semaphore_wait(barrier, len(peers))

    def slot(side, q, j):
        return SLOT[side, 0 if j == 0 else q, j]

    def children(side, q, p):
        return [j for j, parent in TREE[side][q].items() if parent == p]

    def gather_copy(side, q, j, src=None):
        p, s = TREE[side][q][j], slot(side, q, j)
        src = tok.at[slot(side, q, p)] if src is None else src
        return remote(src, tok.at[s], ag_send.at[s], ag_recv.at[s], along(q, j - p))

    def y_tokens():
        s = SLOT[PAR, 0, 0]
        return remote(tokens.at[0], tok.at[s], y_send.at[0], ag_recv.at[s], partner)

    def reduce_copy(side, q, j):
        p, s = TREE[side][q][j], slot(side, q, j)
        src = rs_out if children(side, q, j) else part
        return remote(src.at[s], rs_in.at[s], rs_send.at[s], rs_recv.at[s], along(q, p - j))

    def sum_of(side, j, dirs):
        total = part[slot(side, dirs[0], j)].astype(F32)
        for q in dirs:
            for child in children(side, q, j):
                reduce_copy(side, q, child).wait_recv()
                total = total + rs_in[slot(side, q, child)].astype(F32)
        return total

    y_final = remote(y_out, y_in, y_send.at[1], y_recv.at[0], partner)

    def rows_of(k):
        return pl.ds(pl.multiple_of(k * y_rows, y_rows), y_rows)

    def x_leg(k):
        px = (x + k + 1) % NX
        rows = pl.ds(pl.multiple_of(px * x_rows, x_rows), x_rows)
        return remote(deltas.at[0, rows], x_in.at[k], o_send.at[k], o_recv.at[k], x_peer[k])

    def y_leg(k):
        py = (ylo + k + 1) % NYLO
        return remote(y_mid.at[rows_of(py)], y_sum_in.at[k], o_send.at[3 + k], o_recv.at[3 + k], y_peer[k])

    def y_gather(k):
        rows = rows_of(r)
        return remote(half_all.at[rows], half_all.at[rows], o_send.at[6 + k], o_recv.at[6 + k], y_peer[k])

    def x_gather(k):
        return remote(half_all.at[my_x], half_all.at[my_x], o_send.at[9 + k], o_recv.at[9 + k], x_peer[k])

    def outer(stage):
        if stage == 2:
            loads[4].wait()
            total = delta_v[...].astype(F32)
            for k in range(3):
                x_leg(k).wait_recv()
                total = total + x_in[k].astype(F32)
            y_mid[...] = total.astype(BF16)
            for k in range(3):
                y_leg(k).start()
        elif stage == 3:
            loads[5].wait()
            loads[6].wait()
            total = y_mid[rows_of(ylo), :].astype(F32)
            for k in range(3):
                y_leg(k).wait_recv()
                total = total + y_sum_in[k].astype(F32)
            grad = total / N_REPLICA
            nm = momentum_coef * mom_v[...] + grad
            no = outer_v[...] - outer_rate * (grad + momentum_coef * nm)
            nm_v[...] = nm
            no_v[...] = no
            half_all[rows_of(r), :] = no.astype(BF16)
            for k in range(3):
                y_gather(k).start()
        elif stage == 4:
            for k in range(3):
                y_gather(k).wait_recv()
            for k in range(3):
                x_gather(k).start()
        else:
            for k in range(3):
                x_gather(k).wait_recv()
            merged = mix_weight * up_v[0].astype(F32) + (1.0 - mix_weight) * half_all[...].astype(F32)
            merged_v[...] = merged.astype(BF16)

    weights = [
        remote(src, dst.at[1], w_send.at[k], w_recv.at[k], sibling)
        for k, (src, dst) in enumerate(((gate_w, gate_v), (local_up.at[0], up_v), (down_w, down_v)))
    ]

    def wait_sends(stage):
        if stage == 0:
            for weight in weights:
                weight.wait_send()
            y_tokens().wait_send()
            for side in (OWN, PAR):
                for q in (0, 1):
                    for j in TREE[side][q]:
                        gather_copy(side, q, j).wait_send()
            for k in range(3):
                x_leg(k).wait_send()
                y_leg(k).wait_send()
        elif stage == 1:
            for k in range(3):
                y_gather(k).wait_send()
        else:
            for k in range(3):
                x_gather(k).wait_send()
            for side in (OWN, PAR):
                for q in (0, 1):
                    for j in TREE[side][q]:
                        reduce_copy(side, q, j).wait_send()
            y_final.wait_send()

    def act(kind, *what):
        if kind == "g":
            side, q, j = what
            s = slot(side, q, j)
            gather_copy(side, q, j).wait_recv()
            for child in children(side, q, j):
                gather_copy(side, q, child).start()
        elif kind == "y":
            y_tokens().wait_recv()
            for q in (0, 1):
                for child in children(PAR, q, 0):
                    gather_copy(PAR, q, child).start()
        elif kind == "r":
            side, q, j = what
            if children(side, q, j):
                rs_out[slot(side, q, j)] = sum_of(side, j, (q,)).astype(BF16)
            reduce_copy(side, q, j).start()
        elif kind == "f":
            total = sum_of(what[0], 0, (0, 1))
            if what[0] == PAR:
                y_out[...] = total.astype(BF16)
                y_final.start()
            else:
                y_final.wait_recv()
                out_v[...] = (total + y_in[...].astype(F32)).astype(BF16)
        elif kind == "o":
            outer(what[0])
        else:
            wait_sends(what[0])

    for q in (0, 1):
        for child in children(OWN, q, 0):
            gather_copy(OWN, q, child, tokens.at[0]).start()
    y_tokens().start()
    for weight in weights:
        weight.start()
    for k in range(3):
        x_leg(k).start()
    for load in loads[:4]:
        load.wait()

    blk, width = tok.shape[1], gate_v.shape[2]

    def compute(i, h):
        rows = tok[pl.ds(2 * i, 2)].reshape(2 * blk, ROWS)
        total = jnp.zeros((2 * blk, ROWS), F32)
        for start in range(0, width, 256):
            cols = slice(start, min(start + 256, width))
            gate = jnp.dot(rows, gate_v[h, :, cols], preferred_element_type=F32)
            upper = jnp.dot(rows, up_v[h, :, cols], preferred_element_type=F32)
            hidden = ((gate + gate * jnp.tanh(0.5 * gate)) * upper).astype(BF16)
            total = total + jnp.dot(hidden, down_v[h, cols, :], preferred_element_type=F32)

        @pl.when(h == 0)
        def _():
            acc[...] = total

        @pl.when(h == 1)
        def _():
            both = (acc[...] + total) * (0.5 * ROWS ** -0.5)
            part[pl.ds(2 * i, 2)] = both.astype(BF16).reshape(2, blk, ROWS)

    def unit(u, carry):
        for at, todo in enumerate(BEFORE):
            if todo or at == 1:

                @pl.when(u == at)
                def _():
                    for what in todo:
                        act(*what)
                    if at == 1:
                        for weight in weights:
                            weight.wait_recv()

        compute(u // 2, u % 2)
        return carry

    lax.fori_loop(0, len(BEFORE), unit, 0)
    for what in AFTER:
        act(*what)


def store_kernel(*refs):
    n = (len(refs) - 1) // 2
    copies = [pltpu.make_async_copy(src, dst, refs[-1].at[k]) for k, (src, dst) in enumerate(zip(refs[:n], refs[n:-1]))]
    for copy in copies:
        copy.start()
    for copy in copies:
        copy.wait()


def body(tokens, gate_weight, down_weight, local_up, deltas, outer_up, momentum):
    blk, rows = tokens.shape[1:]
    width = gate_weight.shape[1]
    share = outer_up.shape[0]
    dma = pltpu.SemaphoreType.DMA
    outs = (
        ((blk, rows), BF16, tokens.shape),
        ((ROWS, width), BF16, local_up.shape),
        ((share, width), F32, outer_up.shape),
        ((share, width), F32, momentum.shape),
    )
    args = [
        pltpu.with_memory_space_constraint(arg, pltpu.HBM)
        for arg in (tokens, gate_weight, down_weight, local_up, deltas, outer_up, momentum)
    ]
    held = pl.pallas_call(
        kernel,
        out_shape=tuple(pltpu.VMEM(shape, kind) for shape, kind, _ in outs),
        in_specs=[pl.BlockSpec(memory_space=pltpu.HBM)] * 7,
        out_specs=[pl.BlockSpec(memory_space=pltpu.VMEM)] * 4,
        scratch_shapes=[
            pltpu.VMEM((N_SLOT, blk, rows), BF16),
            pltpu.VMEM((2, ROWS, width), BF16),
            pltpu.VMEM((2, ROWS, width), BF16),
            pltpu.VMEM((2, width, ROWS), BF16),
            pltpu.VMEM((ROWS // NX, width), BF16),
            pltpu.VMEM((share, width), F32),
            pltpu.VMEM((share, width), F32),
            pltpu.VMEM((N_SLOT, blk, rows), BF16),
            pltpu.VMEM((2 * blk, rows), F32),
            pltpu.VMEM((N_SLOT, blk, rows), BF16),
            pltpu.VMEM((N_SLOT, blk, rows), BF16),
            pltpu.VMEM((blk, rows), BF16),
            pltpu.VMEM((blk, rows), BF16),
            pltpu.VMEM((NX - 1, ROWS // NX, width), BF16),
            pltpu.VMEM((ROWS // NX, width), BF16),
            pltpu.VMEM((NYLO - 1, share, width), BF16),
            pltpu.VMEM((ROWS, width), BF16),
            dma((7,)),
            dma((3,)),
            dma((3,)),
            dma((N_SLOT,)),
            dma((N_SLOT,)),
            dma((N_SLOT,)),
            dma((N_SLOT,)),
            dma((2,)),
            dma((1,)),
            dma((12,)),
            dma((12,)),
        ],
        compiler_params=pltpu.CompilerParams(
            collective_id=0, has_side_effects=True, vmem_limit_bytes=32 * 1024 * 1024
        ),
        cost_estimate=pl.CostEstimate(flops=5_700_000_000, bytes_accessed=3_000_000, transcendentals=3_700_000),
    )(*args)
    inner_out, merged_up, new_outer, new_momentum = pl.pallas_call(
        store_kernel,
        out_shape=tuple(jax.ShapeDtypeStruct(shape, kind) for shape, kind, _ in outs),
        in_specs=[pl.BlockSpec(memory_space=pltpu.VMEM)] * 4,
        out_specs=[pl.BlockSpec(memory_space=pl.ANY)] * 4,
        scratch_shapes=[dma((4,))],
        compiler_params=pltpu.CompilerParams(vmem_limit_bytes=1024 * 1024),
    )(*[pltpu.with_memory_space_constraint(part, pltpu.VMEM) for part in held])
    return inner_out[None], merged_up[None], new_outer, new_momentum


def solution(mesh):
    placed = (
        P("replica", "fsdp", None),
        P(None, "fsdp"),
        P("fsdp", None),
        P("replica", None, "fsdp"),
        P("replica", None, "fsdp"),
        P("replica", "fsdp"),
        P("replica", "fsdp"),
    )
    return jax.shard_map(
        body,
        mesh=mesh,
        in_specs=placed,
        out_specs=(
            P("replica", "fsdp", None),
            P("replica", None, "fsdp"),
            P("replica", "fsdp"),
            P("replica", "fsdp"),
        ),
        check_vma=False,
    )
```

```python
import jax
import jax.numpy as jnp
from jax import lax
from jax.experimental import pallas as pl
from jax.experimental.pallas import tpu as pltpu
from jax.sharding import PartitionSpec as P

MESH = pl.DeviceIdType.MESH
BF16, F32 = jnp.bfloat16, jnp.float32

NX, NYLO, NZ = 4, 4, 8
N_REPLICA = NX * NYLO
ROWS = 256

outer_rate = 0.7
momentum_coef = 0.9
mix_weight = 0.5

OWN, PAR = 0, 1
TREE = (
    ({1: 0, 2: 1, 3: 2, 4: 2}, {1: 0, 2: 1, 3: 2}),
    ({1: 0, 2: 0, 3: 2, 4: 2}, {1: 0, 2: 0, 3: 2}),
)
PAIRS = (
    ((0, 0, 0), (0, 0, 1)),
    ((0, 1, 1), (1, 0, 0)),
    ((0, 0, 2), (0, 1, 2)),
    ((1, 0, 1), (1, 1, 1)),
    ((1, 0, 2), (1, 1, 2)),
    ((0, 0, 3), (0, 1, 3)),
    ((1, 0, 4), (1, 0, 3)),
    ((0, 0, 4), (1, 1, 3)),
)
SLOT = {block: 2 * i + k for i, pair in enumerate(PAIRS) for k, block in enumerate(pair)}
N_SLOT = len(SLOT)

BEFORE = (
    (("g", 0, 0, 1),),
    (("g", 0, 1, 1),),
    (("y",),),
    (("g", 0, 0, 2),),
    (("g", 0, 1, 2),),
    (),
    (("g", 1, 0, 1), ("o", 2), ("g", 1, 0, 2), ("g", 1, 1, 1),),
    (),
    (("g", 1, 1, 2), ("r", 1, 0, 1), ("r", 1, 1, 1),),
    (("g", 0, 0, 3),),
    (("g", 0, 0, 4), ("g", 0, 1, 3),),
    (("g", 1, 0, 3), ("o", 3),),
    (("r", 0, 0, 3), ("g", 1, 0, 4), ("r", 0, 1, 3),),
    (("g", 1, 1, 3),),
    (("r", 1, 0, 4), ("r", 1, 0, 3),),
    (),
)
AFTER = (
    ("r", 1, 1, 3),
    ("r", 0, 0, 4),
    ("r", 0, 1, 2),
    ("o", 4),
    ("r", 1, 0, 2),
    ("w", 0),
    ("r", 1, 1, 2),
    ("r", 0, 0, 2),
    ("r", 0, 1, 1),
    ("w", 1),
    ("f", 1),
    ("r", 0, 0, 1),
    ("o", 5),
    ("w", 2),
    ("f", 0),
)


def kernel(
    tokens, gate_w, down_w, local_up, deltas, outer_up, momentum,
    out_v, merged_v, no_v, nm_v,
    tok, gate_v, up_v, down_v, delta_v, outer_v, mom_v,
    part, acc, rs_in, rs_out, y_out, y_in,
    x_in, y_mid, y_sum_in, half_all,
    load_sem, w_send, w_recv, ag_send, ag_recv, rs_send, rs_recv, y_send, y_recv, o_send, o_recv,
):
    r, f = lax.axis_index("replica"), lax.axis_index("fsdp")
    x, ylo = r // NYLO, r % NYLO
    z, yh, c = f // 4, (f // 2) % 2, f % 2
    a = 1 - 2 * c

    def dev(x=x, ylo=ylo, z=z, yh=yh, c=c):
        return (x * NYLO + ylo, z * 4 + yh * 2 + c)

    def along(q, d):
        return dev(z=(z + (a if q == 0 else -a) * d + NZ) % NZ)

    sibling = dev(c=1 - c)
    partner = dev(yh=1 - yh)
    x_peer = [dev(x=(x + k) % NX) for k in range(1, NX)]
    y_peer = [dev(ylo=(ylo + k) % NYLO) for k in range(1, NYLO)]
    steps = sorted({j - p for side in TREE for edges in side for j, p in edges.items()})
    peers = [along(q, d) for d in steps for q in (0, 1)] + [partner, sibling, *x_peer, *y_peer]

    def remote(src, dst, ssem, rsem, to):
        return pltpu.make_async_remote_copy(
            src_ref=src, dst_ref=dst, send_sem=ssem, recv_sem=rsem, device_id=to, device_id_type=MESH
        )

    x_rows = ROWS // NX
    y_rows = ROWS // N_REPLICA
    my_x = pl.ds(pl.multiple_of(x * x_rows, x_rows), x_rows)
    loads = [
        pltpu.make_async_copy(tokens.at[0], tok.at[SLOT[0, 0, 0]], load_sem.at[0]),
        pltpu.make_async_copy(gate_w, gate_v.at[0], load_sem.at[1]),
        pltpu.make_async_copy(local_up.at[0], up_v.at[0], load_sem.at[2]),
        pltpu.make_async_copy(down_w, down_v.at[0], load_sem.at[3]),
        pltpu.make_async_copy(deltas.at[0, my_x], delta_v, load_sem.at[4]),
        pltpu.make_async_copy(outer_up, outer_v, load_sem.at[5]),
        pltpu.make_async_copy(momentum, mom_v, load_sem.at[6]),
    ]
    barrier = pltpu.get_barrier_semaphore()
    for peer in peers:
        pl.semaphore_signal(barrier, inc=1, device_id=peer, device_id_type=MESH)
    for load in loads:
        load.start()
    pl.semaphore_wait(barrier, len(peers))

    def slot(side, q, j):
        return SLOT[side, 0 if j == 0 else q, j]

    def children(side, q, p):
        return [j for j, parent in TREE[side][q].items() if parent == p]

    def gather_copy(side, q, j, src=None):
        p, s = TREE[side][q][j], slot(side, q, j)
        src = tok.at[slot(side, q, p)] if src is None else src
        return remote(src, tok.at[s], ag_send.at[s], ag_recv.at[s], along(q, j - p))

    def y_tokens():
        s = SLOT[PAR, 0, 0]
        return remote(tokens.at[0], tok.at[s], y_send.at[0], ag_recv.at[s], partner)

    def reduce_copy(side, q, j):
        p, s = TREE[side][q][j], slot(side, q, j)
        src = rs_out if children(side, q, j) else part
        return remote(src.at[s], rs_in.at[s], rs_send.at[s], rs_recv.at[s], along(q, p - j))

    def in_rows(n, size, work):
        def turn(i, carry):
            work(pl.ds(pl.multiple_of(i * size, size), size))
            return carry

        lax.fori_loop(0, n, turn, 0)

    def sum_into(side, j, dirs, store):
        held = [(q, child) for q in dirs for child in children(side, q, j)]
        for q, child in held:
            reduce_copy(side, q, child).wait_recv()

        def work(rows):
            total = part[slot(side, dirs[0], j), rows, :].astype(F32)
            for q, child in held:
                total = total + rs_in[slot(side, q, child), rows, :].astype(F32)
            store(rows, total)

        in_rows(4, tok.shape[1] // 4, work)

    y_final = remote(y_out, y_in, y_send.at[1], y_recv.at[0], partner)

    def rows_of(k):
        return pl.ds(pl.multiple_of(k * y_rows, y_rows), y_rows)

    def x_leg(k):
        px = (x + k + 1) % NX
        rows = pl.ds(pl.multiple_of(px * x_rows, x_rows), x_rows)
        return remote(deltas.at[0, rows], x_in.at[k], o_send.at[k], o_recv.at[k], x_peer[k])

    def y_leg(k):
        py = (ylo + k + 1) % NYLO
        return remote(y_mid.at[rows_of(py)], y_sum_in.at[k], o_send.at[3 + k], o_recv.at[3 + k], y_peer[k])

    def y_gather(k):
        rows = rows_of(r)
        return remote(half_all.at[rows], half_all.at[rows], o_send.at[6 + k], o_recv.at[6 + k], y_peer[k])

    def x_gather(k):
        return remote(half_all.at[my_x], half_all.at[my_x], o_send.at[9 + k], o_recv.at[9 + k], x_peer[k])

    def outer(stage):
        if stage == 2:
            loads[4].wait()
            for k in range(3):
                x_leg(k).wait_recv()

            def work(rows):
                total = delta_v[rows, :].astype(F32)
                for k in range(3):
                    total = total + x_in[k, rows, :].astype(F32)
                y_mid[rows, :] = total.astype(BF16)

            in_rows(4, x_rows // 4, work)
            for k in range(3):
                y_leg(k).start()
        elif stage == 3:
            loads[5].wait()
            loads[6].wait()
            total = y_mid[rows_of(ylo), :].astype(F32)
            for k in range(3):
                y_leg(k).wait_recv()
                total = total + y_sum_in[k].astype(F32)
            grad = total / N_REPLICA
            nm = momentum_coef * mom_v[...] + grad
            no = outer_v[...] - outer_rate * (grad + momentum_coef * nm)
            nm_v[...] = nm
            no_v[...] = no
            half_all[rows_of(r), :] = no.astype(BF16)
            for k in range(3):
                y_gather(k).start()
        elif stage == 4:
            for k in range(3):
                y_gather(k).wait_recv()
            for k in range(3):
                x_gather(k).start()
        else:
            for k in range(3):
                x_gather(k).wait_recv()

            def work(rows):
                merged = mix_weight * up_v[0, rows, :].astype(F32) + (1.0 - mix_weight) * half_all[rows, :].astype(F32)
                merged_v[rows, :] = merged.astype(BF16)

            in_rows(16, ROWS // 16, work)

    weights = [
        remote(src, dst.at[1], w_send.at[k], w_recv.at[k], sibling)
        for k, (src, dst) in enumerate(((gate_w, gate_v), (local_up.at[0], up_v), (down_w, down_v)))
    ]

    def sent_all(held, sem):
        first, second = sorted((SLOT[OWN, 0, 0], SLOT[PAR, 0, 0]))

        def turn(s, carry):
            remote(held.at[s], held.at[s], sem.at[s], sem.at[s], partner).wait_send()
            return carry

        for low, high in ((0, first), (first + 1, second), (second + 1, N_SLOT)):
            if low < high:
                lax.fori_loop(low, high, turn, 0)

    def wait_sends(stage):
        if stage == 0:
            for weight in weights:
                weight.wait_send()
            y_tokens().wait_send()
            sent_all(tok, ag_send)
            for k in range(3):
                x_leg(k).wait_send()
                y_leg(k).wait_send()
        elif stage == 1:
            for k in range(3):
                y_gather(k).wait_send()
        else:
            for k in range(3):
                x_gather(k).wait_send()
            sent_all(part, rs_send)
            y_final.wait_send()

    def act(kind, *what):
        if kind == "g":
            side, q, j = what
            s = slot(side, q, j)
            gather_copy(side, q, j).wait_recv()
            for child in children(side, q, j):
                gather_copy(side, q, child).start()
        elif kind == "y":
            y_tokens().wait_recv()
            for q in (0, 1):
                for child in children(PAR, q, 0):
                    gather_copy(PAR, q, child).start()
        elif kind == "r":
            side, q, j = what
            if children(side, q, j):


                def store(rows, total):
                    rs_out[slot(side, q, j), rows, :] = total.astype(BF16)

                sum_into(side, j, (q,), store)
            reduce_copy(side, q, j).start()
        elif kind == "f":
            if what[0] == PAR:

                def store(rows, total):
                    y_out[rows, :] = total.astype(BF16)

                sum_into(PAR, 0, (0, 1), store)
                y_final.start()
            else:

                def store(rows, total):
                    out_v[rows, :] = (total + y_in[rows, :].astype(F32)).astype(BF16)

                y_final.wait_recv()
                sum_into(OWN, 0, (0, 1), store)
        elif kind == "o":
            outer(what[0])
        else:
            wait_sends(what[0])

    for q in (0, 1):
        for child in children(OWN, q, 0):
            gather_copy(OWN, q, child, tokens.at[0]).start()
    y_tokens().start()
    for weight in weights:
        weight.start()
    for k in range(3):
        x_leg(k).start()
    for load in loads[:4]:
        load.wait()

    blk, width = tok.shape[1], gate_v.shape[2]

    def compute(i, h):
        rows = tok[pl.ds(2 * i, 2)].reshape(2 * blk, ROWS)
        total = jnp.zeros((2 * blk, ROWS), F32)
        for start in range(0, width, 256):
            cols = slice(start, min(start + 256, width))
            gate = jnp.dot(rows, gate_v[h, :, cols], preferred_element_type=F32)
            upper = jnp.dot(rows, up_v[h, :, cols], preferred_element_type=F32)
            hidden = ((gate + gate * jnp.tanh(0.5 * gate)) * upper).astype(BF16)
            total = total + jnp.dot(hidden, down_v[h, cols, :], preferred_element_type=F32)

        @pl.when(h == 0)
        def _():
            acc[...] = total

        @pl.when(h == 1)
        def _():
            both = (acc[...] + total) * (0.5 * ROWS ** -0.5)
            part[pl.ds(2 * i, 2)] = both.astype(BF16).reshape(2, blk, ROWS)

    def prepare(at):
        for what in BEFORE[at]:
            act(*what)
        if at == 1:
            for weight in weights:
                weight.wait_recv()

    def dispatch(u, low, high):
        if high - low == 1:
            prepare(low)
            return
        middle = (low + high) // 2
        lax.cond(u < middle, lambda: dispatch(u, low, middle), lambda: dispatch(u, middle, high))

    def unit(u, carry):
        dispatch(u, 0, len(BEFORE))
        compute(u // 2, u % 2)
        return carry

    lax.fori_loop(0, len(BEFORE), unit, 0)
    for what in AFTER:
        act(*what)


def store_kernel(*refs):
    n = (len(refs) - 1) // 2
    copies = [pltpu.make_async_copy(src, dst, refs[-1].at[k]) for k, (src, dst) in enumerate(zip(refs[:n], refs[n:-1]))]
    for copy in copies:
        copy.start()
    for copy in copies:
        copy.wait()


def body(tokens, gate_weight, down_weight, local_up, deltas, outer_up, momentum):
    blk, rows = tokens.shape[1:]
    width = gate_weight.shape[1]
    share = outer_up.shape[0]
    dma = pltpu.SemaphoreType.DMA
    outs = (
        ((blk, rows), BF16, tokens.shape),
        ((ROWS, width), BF16, local_up.shape),
        ((share, width), F32, outer_up.shape),
        ((share, width), F32, momentum.shape),
    )
    args = [
        pltpu.with_memory_space_constraint(arg, pltpu.HBM)
        for arg in (tokens, gate_weight, down_weight, local_up, deltas, outer_up, momentum)
    ]
    held = pl.pallas_call(
        kernel,
        out_shape=tuple(pltpu.VMEM(shape, kind) for shape, kind, _ in outs),
        in_specs=[pl.BlockSpec(memory_space=pltpu.HBM)] * 7,
        out_specs=[pl.BlockSpec(memory_space=pltpu.VMEM)] * 4,
        scratch_shapes=[
            pltpu.VMEM((N_SLOT, blk, rows), BF16),
            pltpu.VMEM((2, ROWS, width), BF16),
            pltpu.VMEM((2, ROWS, width), BF16),
            pltpu.VMEM((2, width, ROWS), BF16),
            pltpu.VMEM((ROWS // NX, width), BF16),
            pltpu.VMEM((share, width), F32),
            pltpu.VMEM((share, width), F32),
            pltpu.VMEM((N_SLOT, blk, rows), BF16),
            pltpu.VMEM((2 * blk, rows), F32),
            pltpu.VMEM((N_SLOT, blk, rows), BF16),
            pltpu.VMEM((N_SLOT, blk, rows), BF16),
            pltpu.VMEM((blk, rows), BF16),
            pltpu.VMEM((blk, rows), BF16),
            pltpu.VMEM((NX - 1, ROWS // NX, width), BF16),
            pltpu.VMEM((ROWS // NX, width), BF16),
            pltpu.VMEM((NYLO - 1, share, width), BF16),
            pltpu.VMEM((ROWS, width), BF16),
            dma((7,)),
            dma((3,)),
            dma((3,)),
            dma((N_SLOT,)),
            dma((N_SLOT,)),
            dma((N_SLOT,)),
            dma((N_SLOT,)),
            dma((2,)),
            dma((1,)),
            dma((12,)),
            dma((12,)),
        ],
        compiler_params=pltpu.CompilerParams(
            collective_id=0, has_side_effects=True, vmem_limit_bytes=32 * 1024 * 1024
        ),
        cost_estimate=pl.CostEstimate(flops=5_700_000_000, bytes_accessed=3_000_000, transcendentals=3_700_000),
    )(*args)
    inner_out, merged_up, new_outer, new_momentum = pl.pallas_call(
        store_kernel,
        out_shape=tuple(jax.ShapeDtypeStruct(shape, kind) for shape, kind, _ in outs),
        in_specs=[pl.BlockSpec(memory_space=pltpu.VMEM)] * 4,
        out_specs=[pl.BlockSpec(memory_space=pl.ANY)] * 4,
        scratch_shapes=[dma((4,))],
        compiler_params=pltpu.CompilerParams(vmem_limit_bytes=1024 * 1024),
    )(*[pltpu.with_memory_space_constraint(part, pltpu.VMEM) for part in held])
    return inner_out[None], merged_up[None], new_outer, new_momentum


def solution(mesh):
    placed = (
        P("replica", "fsdp", None),
        P(None, "fsdp"),
        P("fsdp", None),
        P("replica", None, "fsdp"),
        P("replica", None, "fsdp"),
        P("replica", "fsdp"),
        P("replica", "fsdp"),
    )
    return jax.shard_map(
        body,
        mesh=mesh,
        in_specs=placed,
        out_specs=(
            P("replica", "fsdp", None),
            P("replica", None, "fsdp"),
            P("replica", "fsdp"),
            P("replica", "fsdp"),
        ),
        check_vma=False,
    )
```

```python
import jax
import jax.numpy as jnp
from jax import lax
from jax.experimental import pallas as pl
from jax.experimental.pallas import tpu as pltpu
from jax.sharding import PartitionSpec as P

MESH = pl.DeviceIdType.MESH
BF16, F32 = jnp.bfloat16, jnp.float32

NX, NYLO, NZ = 4, 4, 8
N_REPLICA = NX * NYLO
ROWS = 256

outer_rate = 0.7
momentum_coef = 0.9
mix_weight = 0.5

OWN, PAR = 0, 1


def hop(p, e):
    d = (e - p) % NZ
    return d - NZ if d > NZ // 2 else d


TREE = (
    (
        {1: 0, 2: 1, 3: 2, 4: 2, -1: 0, -2: -1, -3: -2},
        {1: 0, 2: 0, 3: 2, 4: 2, -1: 0, -2: 0, -3: -2},
    ),
    (
        {1: 0, 2: 1, 3: 2, 4: 3, -1: 0, -2: -1, -3: -2},
        {1: 0, 2: 0, 3: 2, 4: 2, -1: 0, -2: 0, -3: -2},
    ),
)
PAIRS = (
    (
        ((0, 0), (0, 1)),
        ((0, -1), (1, 0)),
        ((0, 2), (0, -2)),
        ((1, 1), (1, -1)),
        ((1, 2), (1, -2)),
        ((0, 3), (0, -3)),
        ((1, 4), (1, 3)),
        ((0, 4), (1, -3)),
    ),
    (
        ((0, 0), (0, 1)),
        ((0, -1), (1, 0)),
        ((0, 2), (0, -2)),
        ((1, 1), (1, -1)),
        ((1, 2), (1, -2)),
        ((0, 3), (0, -3)),
        ((1, 4), (1, 3)),
        ((0, 4), (1, -3)),
    ),
)
SLOT = [{block: 2 * i + k for i, pair in enumerate(pairs) for k, block in enumerate(pair)} for pairs in PAIRS]
N_SLOT = len(SLOT[0])

BEFORE = (
    (
        (("g", 0, 1),),
        (("g", 0, -1),),
        (("g", 1, 0),),
        (("g", 0, 2),),
        (("g", 0, -2),),
        (),
        (("g", 1, 1), ("o", 2), ("g", 1, 2), ("g", 1, -1),),
        (),
        (("g", 1, -2), ("r", 1, 1), ("r", 1, -1),),
        (("g", 0, 3),),
        (("g", 0, 4), ("g", 0, -3),),
        (("g", 1, 3), ("o", 3),),
        (("r", 0, 3), ("g", 1, 4), ("r", 0, -3),),
        (("g", 1, -3),),
        (("r", 1, 4), ("r", 1, 3),),
        (),
    ),
    (
        (("g", 0, 1), ("g", 0, -1), ("g", 1, 0),),
        (),
        (),
        (),
        (("g", 0, 2), ("g", 0, -2),),
        (("o", 2),),
        (("g", 1, 1), ("g", 1, 2), ("g", 1, -1),),
        (),
        (("g", 1, -2),),
        (),
        (("g", 0, 3), ("r", 1, 1), ("r", 1, -1), ("g", 0, -3),),
        (),
        (("r", 0, -3), ("o", 3), ("g", 1, 3), ("g", 1, 4),),
        (),
        (("r", 1, 4), ("g", 1, -3), ("g", 0, 4),),
        (),
    ),
)
AFTER = (
    (
        ("r", 1, -3),
        ("r", 0, 4),
        ("r", 0, -2),
        ("o", 4),
        ("r", 1, 2),
        ("w", 0),
        ("r", 1, -2),
        ("r", 0, 2),
        ("r", 0, -1),
        ("f", 1),
        ("r", 0, 1),
        ("o", 5),
        ("w", 1),
        ("w", 2),
        ("f", 0),
    ),
    (
        ("r", 0, 4),
        ("r", 1, 3),
        ("r", 1, -3),
        ("r", 0, -2),
        ("r", 0, 3),
        ("r", 1, 2),
        ("o", 4),
        ("w", 0),
        ("r", 1, -2),
        ("r", 0, 2),
        ("r", 0, -1),
        ("f", 1),
        ("r", 0, 1),
        ("o", 5),
        ("w", 1),
        ("w", 2),
        ("f", 0),
    ),
)


def kernel(
    tokens, gate_w, down_w, local_up, deltas, outer_up, momentum,
    out_v, merged_v, no_v, nm_v,
    tok, gate_v, up_v, down_v, delta_v, outer_v, mom_v,
    part, acc, rs_in, rs_out, y_out, y_in,
    x_in, y_mid, y_sum_in, half_all,
    load_sem, w_send, w_recv, ag_send, ag_recv, rs_send, rs_recv, y_send, y_recv, o_send, o_recv,
):
    r, f = lax.axis_index("replica"), lax.axis_index("fsdp")
    x, ylo = r // NYLO, r % NYLO
    z, yh, c = f // 4, (f // 2) % 2, f % 2
    a = 1 - 2 * c

    def dev(x=x, ylo=ylo, z=z, yh=yh, c=c):
        return (x * NYLO + ylo, z * 4 + yh * 2 + c)

    def along(d):
        return dev(z=(z + a * d + NZ) % NZ)

    sibling = dev(c=1 - c)
    partner = dev(yh=1 - yh)
    x_peer = [dev(x=(x + k) % NX) for k in range(1, NX)]
    y_peer = [dev(ylo=(ylo + k) % NYLO) for k in range(1, NYLO)]
    steps = {abs(hop(p, e)) for core in TREE for tree in core for e, p in tree.items()}
    peers = [along(d) for k in sorted(steps) for d in (k, -k)] + [partner, sibling, *x_peer, *y_peer]

    def remote(src, dst, ssem, rsem, to):
        return pltpu.make_async_remote_copy(
            src_ref=src, dst_ref=dst, send_sem=ssem, recv_sem=rsem, device_id=to, device_id_type=MESH
        )

    x_rows = ROWS // NX
    y_rows = ROWS // N_REPLICA
    my_x = pl.ds(pl.multiple_of(x * x_rows, x_rows), x_rows)
    loads = [
        pltpu.make_async_copy(tokens.at[0], tok.at[SLOT[0][OWN, 0]], load_sem.at[0]),
        pltpu.make_async_copy(gate_w, gate_v.at[0], load_sem.at[1]),
        pltpu.make_async_copy(local_up.at[0], up_v.at[0], load_sem.at[2]),
        pltpu.make_async_copy(down_w, down_v.at[0], load_sem.at[3]),
        pltpu.make_async_copy(deltas.at[0, my_x], delta_v, load_sem.at[4]),
        pltpu.make_async_copy(outer_up, outer_v, load_sem.at[5]),
        pltpu.make_async_copy(momentum, mom_v, load_sem.at[6]),
    ]
    barrier = pltpu.get_barrier_semaphore()
    for peer in peers:
        pl.semaphore_signal(barrier, inc=1, device_id=peer, device_id_type=MESH)
    for load in loads:
        load.start()
    pl.semaphore_wait(barrier, len(peers))

    def children(core, side, p):
        return [e for e, parent in TREE[core][side].items() if parent == p]

    def gather_copy(core, side, e, src=None):
        p, s = TREE[core][side][e], SLOT[core][side, e]
        src = tok.at[SLOT[core][side, p]] if src is None else src
        return remote(src, tok.at[s], ag_send.at[s], ag_recv.at[s], along(hop(p, e)))

    def y_tokens(core):
        s = SLOT[core][PAR, 0]
        return remote(tokens.at[0], tok.at[s], y_send.at[0], ag_recv.at[s], partner)

    def reduce_copy(core, side, e):
        p, s = TREE[core][side][e], SLOT[core][side, e]
        src = rs_out if children(core, side, e) else part
        return remote(src.at[s], rs_in.at[s], rs_send.at[s], rs_recv.at[s], along(-hop(p, e)))

    def in_rows(n, size, work):
        def turn(i, carry):
            work(pl.ds(pl.multiple_of(i * size, size), size))
            return carry

        lax.fori_loop(0, n, turn, 0)

    def sum_into(core, side, e, store):
        held = children(core, side, e)
        for child in held:
            reduce_copy(core, side, child).wait_recv()

        def work(rows):
            total = part[SLOT[core][side, e], rows, :].astype(F32)
            for child in held:
                total = total + rs_in[SLOT[core][side, child], rows, :].astype(F32)
            store(rows, total)

        in_rows(4, tok.shape[1] // 4, work)

    y_final = remote(y_out, y_in, y_send.at[1], y_recv.at[0], partner)

    def rows_of(k):
        return pl.ds(pl.multiple_of(k * y_rows, y_rows), y_rows)

    def x_leg(k):
        px = (x + k + 1) % NX
        rows = pl.ds(pl.multiple_of(px * x_rows, x_rows), x_rows)
        return remote(deltas.at[0, rows], x_in.at[k], o_send.at[k], o_recv.at[k], x_peer[k])

    def y_leg(k):
        py = (ylo + k + 1) % NYLO
        return remote(y_mid.at[rows_of(py)], y_sum_in.at[k], o_send.at[3 + k], o_recv.at[3 + k], y_peer[k])

    def y_gather(k):
        rows = rows_of(r)
        return remote(half_all.at[rows], half_all.at[rows], o_send.at[6 + k], o_recv.at[6 + k], y_peer[k])

    def x_gather(k):
        return remote(half_all.at[my_x], half_all.at[my_x], o_send.at[9 + k], o_recv.at[9 + k], x_peer[k])

    def outer(stage):
        if stage == 2:
            loads[4].wait()
            for k in range(3):
                x_leg(k).wait_recv()

            def work(rows):
                total = delta_v[rows, :].astype(F32)
                for k in range(3):
                    total = total + x_in[k, rows, :].astype(F32)
                y_mid[rows, :] = total.astype(BF16)

            in_rows(4, x_rows // 4, work)
            for k in range(3):
                y_leg(k).start()
        elif stage == 3:
            loads[5].wait()
            loads[6].wait()
            total = y_mid[rows_of(ylo), :].astype(F32)
            for k in range(3):
                y_leg(k).wait_recv()
                total = total + y_sum_in[k].astype(F32)
            grad = total / N_REPLICA
            nm = momentum_coef * mom_v[...] + grad
            no = outer_v[...] - outer_rate * (grad + momentum_coef * nm)
            nm_v[...] = nm
            no_v[...] = no
            half_all[rows_of(r), :] = no.astype(BF16)
            for k in range(3):
                y_gather(k).start()
        elif stage == 4:
            for k in range(3):
                y_gather(k).wait_recv()
            for k in range(3):
                x_gather(k).start()
        else:
            for k in range(3):
                x_gather(k).wait_recv()

            def work(rows):
                merged = mix_weight * up_v[0, rows, :].astype(F32) + (1.0 - mix_weight) * half_all[rows, :].astype(F32)
                merged_v[rows, :] = merged.astype(BF16)

            in_rows(16, ROWS // 16, work)

    weights = [
        remote(src, dst.at[1], w_send.at[k], w_recv.at[k], sibling)
        for k, (src, dst) in enumerate(((gate_w, gate_v), (local_up.at[0], up_v), (down_w, down_v)))
    ]

    def sent_all(core, held, sem):
        first, second = sorted((SLOT[core][OWN, 0], SLOT[core][PAR, 0]))

        def turn(s, carry):
            remote(held.at[s], held.at[s], sem.at[s], sem.at[s], partner).wait_send()
            return carry

        for low, high in ((0, first), (first + 1, second), (second + 1, N_SLOT)):
            if low < high:
                lax.fori_loop(low, high, turn, 0)

    def wait_sends(core, stage):
        if stage == 0:
            for weight in weights:
                weight.wait_send()
            y_tokens(core).wait_send()
            sent_all(core, tok, ag_send)
            for k in range(3):
                x_leg(k).wait_send()
                y_leg(k).wait_send()
        elif stage == 1:
            for k in range(3):
                y_gather(k).wait_send()
        else:
            for k in range(3):
                x_gather(k).wait_send()
            sent_all(core, part, rs_send)
            y_final.wait_send()

    def act(core, kind, *what):
        if kind == "g":
            side, e = what
            copy = gather_copy(core, side, e) if e else y_tokens(core)
            copy.wait_recv()
            for child in children(core, side, e):
                gather_copy(core, side, child).start()
        elif kind == "r":
            side, e = what
            if children(core, side, e):


                def store(rows, total):
                    rs_out[SLOT[core][side, e], rows, :] = total.astype(BF16)

                sum_into(core, side, e, store)
            reduce_copy(core, side, e).start()
        elif kind == "f":
            if what[0] == PAR:

                def store(rows, total):
                    y_out[rows, :] = total.astype(BF16)

                sum_into(core, PAR, 0, store)
                y_final.start()
            else:

                def store(rows, total):
                    out_v[rows, :] = (total + y_in[rows, :].astype(F32)).astype(BF16)

                y_final.wait_recv()
                sum_into(core, OWN, 0, store)
        elif kind == "o":
            outer(what[0])
        else:
            wait_sends(core, what[0])

    for core in (0, 1):

        @pl.when(c == core)
        def _():
            for child in children(core, OWN, 0):
                gather_copy(core, OWN, child, tokens.at[0]).start()
            y_tokens(core).start()

    for weight in weights:
        weight.start()
    for k in range(3):
        x_leg(k).start()
    for load in loads[:4]:
        load.wait()

    blk, width = tok.shape[1], gate_v.shape[2]

    def compute(i, h):
        rows = tok[pl.ds(2 * i, 2)].reshape(2 * blk, ROWS)
        total = jnp.zeros((2 * blk, ROWS), F32)
        for start in range(0, width, 256):
            cols = slice(start, min(start + 256, width))
            gate = jnp.dot(rows, gate_v[h, :, cols], preferred_element_type=F32)
            upper = jnp.dot(rows, up_v[h, :, cols], preferred_element_type=F32)
            hidden = ((gate + gate * jnp.tanh(0.5 * gate)) * upper).astype(BF16)
            total = total + jnp.dot(hidden, down_v[h, cols, :], preferred_element_type=F32)

        @pl.when(h == 0)
        def _():
            acc[...] = total

        @pl.when(h == 1)
        def _():
            both = (acc[...] + total) * (0.5 * ROWS ** -0.5)
            part[pl.ds(2 * i, 2)] = both.astype(BF16).reshape(2, blk, ROWS)

    def each(todo):
        for core in (0, 1):
            if todo[core]:

                @pl.when(c == core)
                def _():
                    for what in todo[core]:
                        act(core, *what)

    def prepare(at):
        each([BEFORE[core][at] for core in (0, 1)])
        if at == 1:
            for weight in weights:
                weight.wait_recv()

    def dispatch(u, low, high):
        if high - low == 1:
            prepare(low)
            return
        middle = (low + high) // 2
        lax.cond(u < middle, lambda: dispatch(u, low, middle), lambda: dispatch(u, middle, high))

    def unit(u, carry):
        dispatch(u, 0, N_SLOT)
        compute(u // 2, u % 2)
        return carry

    lax.fori_loop(0, N_SLOT, unit, 0)
    each(AFTER)


def store_kernel(*refs):
    n = (len(refs) - 1) // 2
    copies = [pltpu.make_async_copy(src, dst, refs[-1].at[k]) for k, (src, dst) in enumerate(zip(refs[:n], refs[n:-1]))]
    for copy in copies:
        copy.start()
    for copy in copies:
        copy.wait()


def body(tokens, gate_weight, down_weight, local_up, deltas, outer_up, momentum):
    blk, rows = tokens.shape[1:]
    width = gate_weight.shape[1]
    share = outer_up.shape[0]
    dma = pltpu.SemaphoreType.DMA
    outs = (
        ((blk, rows), BF16, tokens.shape),
        ((ROWS, width), BF16, local_up.shape),
        ((share, width), F32, outer_up.shape),
        ((share, width), F32, momentum.shape),
    )
    args = [
        pltpu.with_memory_space_constraint(arg, pltpu.HBM)
        for arg in (tokens, gate_weight, down_weight, local_up, deltas, outer_up, momentum)
    ]
    held = pl.pallas_call(
        kernel,
        out_shape=tuple(pltpu.VMEM(shape, kind) for shape, kind, _ in outs),
        in_specs=[pl.BlockSpec(memory_space=pltpu.HBM)] * 7,
        out_specs=[pl.BlockSpec(memory_space=pltpu.VMEM)] * 4,
        scratch_shapes=[
            pltpu.VMEM((N_SLOT, blk, rows), BF16),
            pltpu.VMEM((2, ROWS, width), BF16),
            pltpu.VMEM((2, ROWS, width), BF16),
            pltpu.VMEM((2, width, ROWS), BF16),
            pltpu.VMEM((ROWS // NX, width), BF16),
            pltpu.VMEM((share, width), F32),
            pltpu.VMEM((share, width), F32),
            pltpu.VMEM((N_SLOT, blk, rows), BF16),
            pltpu.VMEM((2 * blk, rows), F32),
            pltpu.VMEM((N_SLOT, blk, rows), BF16),
            pltpu.VMEM((N_SLOT, blk, rows), BF16),
            pltpu.VMEM((blk, rows), BF16),
            pltpu.VMEM((blk, rows), BF16),
            pltpu.VMEM((NX - 1, ROWS // NX, width), BF16),
            pltpu.VMEM((ROWS // NX, width), BF16),
            pltpu.VMEM((NYLO - 1, share, width), BF16),
            pltpu.VMEM((ROWS, width), BF16),
            dma((7,)),
            dma((3,)),
            dma((3,)),
            dma((N_SLOT,)),
            dma((N_SLOT,)),
            dma((N_SLOT,)),
            dma((N_SLOT,)),
            dma((2,)),
            dma((1,)),
            dma((12,)),
            dma((12,)),
        ],
        compiler_params=pltpu.CompilerParams(
            collective_id=0, has_side_effects=True, vmem_limit_bytes=32 * 1024 * 1024
        ),
        cost_estimate=pl.CostEstimate(flops=5_700_000_000, bytes_accessed=3_000_000, transcendentals=3_700_000),
    )(*args)
    inner_out, merged_up, new_outer, new_momentum = pl.pallas_call(
        store_kernel,
        out_shape=tuple(jax.ShapeDtypeStruct(shape, kind) for shape, kind, _ in outs),
        in_specs=[pl.BlockSpec(memory_space=pltpu.VMEM)] * 4,
        out_specs=[pl.BlockSpec(memory_space=pl.ANY)] * 4,
        scratch_shapes=[dma((4,))],
        compiler_params=pltpu.CompilerParams(vmem_limit_bytes=1024 * 1024),
    )(*[pltpu.with_memory_space_constraint(part, pltpu.VMEM) for part in held])
    return inner_out[None], merged_up[None], new_outer, new_momentum


def solution(mesh):
    placed = (
        P("replica", "fsdp", None),
        P(None, "fsdp"),
        P("fsdp", None),
        P("replica", None, "fsdp"),
        P("replica", None, "fsdp"),
        P("replica", "fsdp"),
        P("replica", "fsdp"),
    )
    return jax.shard_map(
        body,
        mesh=mesh,
        in_specs=placed,
        out_specs=(
            P("replica", "fsdp", None),
            P("replica", None, "fsdp"),
            P("replica", "fsdp"),
            P("replica", "fsdp"),
        ),
        check_vma=False,
    )
```

```python
import jax
import jax.numpy as jnp
from jax import lax
from jax.experimental import pallas as pl
from jax.experimental.pallas import tpu as pltpu
from jax.sharding import PartitionSpec as P

MESH = pl.DeviceIdType.MESH
BF16, F32 = jnp.bfloat16, jnp.float32

NX, NYLO, NZ = 4, 4, 8
N_REPLICA = NX * NYLO
ROWS = 256

outer_rate = 0.7
momentum_coef = 0.9
mix_weight = 0.5

OWN, PAR = 0, 1


def hop(p, e):
    d = (e - p) % NZ
    return d - NZ if d > NZ // 2 else d


TREE = (
    (
        {1: 0, 2: 1, 3: 2, 4: 2, -1: 0, -2: -1, -3: -2},
        {1: 0, 2: 0, 3: 2, 4: 2, -1: 0, -2: 0, -3: -2},
    ),
    (
        {1: 0, 2: 1, 3: 2, 4: 3, -1: 0, -2: -1, -3: -2},
        {1: 0, 2: 0, 3: 2, 4: 2, -1: 0, -2: 0, -3: -2},
    ),
)
PAIRS = (
    (
        ((0, 0), (0, 1)),
        ((0, -1), (1, 0)),
        ((0, 2), (0, -2)),
        ((1, 1), (1, -1)),
        ((1, 2), (1, -2)),
        ((0, 3), (0, -3)),
        ((1, 4), (1, 3)),
        ((0, 4), (1, -3)),
    ),
    (
        ((0, 0), (0, 1)),
        ((0, -1), (1, 0)),
        ((0, 2), (0, -2)),
        ((1, 1), (1, -1)),
        ((1, 2), (1, -2)),
        ((0, 3), (0, -3)),
        ((1, 4), (1, 3)),
        ((0, 4), (1, -3)),
    ),
)
SLOT = [{block: 2 * i + k for i, pair in enumerate(pairs) for k, block in enumerate(pair)} for pairs in PAIRS]
N_SLOT = len(SLOT[0])

BEFORE = (
    (
        (("g", 0, 1), ("g", 0, -1),),
        (),
        (("g", 1, 0),),
        (("g", 0, 2),),
        (("g", 0, -2),),
        (),
        (("g", 1, 1), ("o", 2), ("g", 1, 2), ("g", 1, -1),),
        (),
        (("g", 1, -2), ("r", 1, 1), ("r", 1, -1),),
        (("g", 0, 3),),
        (("g", 0, 4), ("g", 0, -3),),
        (("g", 1, 3), ("o", 3),),
        (("r", 0, 3), ("g", 1, 4), ("r", 0, -3),),
        (("g", 1, -3),),
        (("r", 1, 4), ("r", 1, 3),),
        (),
    ),
    (
        (("g", 0, 1), ("g", 0, -1), ("g", 1, 0),),
        (),
        (),
        (),
        (("g", 0, 2), ("g", 0, -2),),
        (("o", 2),),
        (("g", 1, 1), ("g", 1, 2), ("g", 1, -1),),
        (),
        (("g", 1, -2),),
        (),
        (("g", 0, 3), ("r", 1, 1), ("r", 1, -1), ("g", 0, -3),),
        (),
        (("r", 0, -3), ("o", 3), ("g", 1, 3), ("g", 1, 4),),
        (),
        (("r", 1, 4), ("g", 1, -3), ("g", 0, 4),),
        (),
    ),
)
AFTER = (
    (
        ("r", 1, -3),
        ("r", 0, 4),
        ("r", 0, -2),
        ("o", 4),
        ("r", 1, 2),
        ("r", 1, -2),
        ("r", 0, 2),
        ("r", 0, -1),
        ("f", 1),
        ("w", 0),
        ("r", 0, 1),
        ("o", 5),
        ("w", 1),
        ("w", 2),
        ("f", 0),
    ),
    (
        ("r", 0, 4),
        ("r", 1, 3),
        ("r", 1, -3),
        ("r", 0, -2),
        ("r", 0, 3),
        ("r", 1, 2),
        ("o", 4),
        ("r", 1, -2),
        ("r", 0, 2),
        ("r", 0, -1),
        ("f", 1),
        ("w", 0),
        ("r", 0, 1),
        ("o", 5),
        ("w", 1),
        ("w", 2),
        ("f", 0),
    ),
)


def kernel(
    tokens, gate_w, down_w, local_up, deltas, outer_up, momentum,
    out_v, merged_v, no_v, nm_v,
    tok, gate_v, up_v, down_v, delta_v, outer_v, mom_v,
    part, acc, rs_in, rs_out, y_out, y_in,
    x_in, y_mid, y_sum_in, half_all,
    load_sem, w_send, w_recv, ag_send, ag_recv, rs_send, rs_recv, y_send, y_recv, o_send, o_recv,
):
    r, f = lax.axis_index("replica"), lax.axis_index("fsdp")
    x, ylo = r // NYLO, r % NYLO
    z, yh, c = f // 4, (f // 2) % 2, f % 2
    a = 1 - 2 * c

    def dev(x=x, ylo=ylo, z=z, yh=yh, c=c):
        return (x * NYLO + ylo, z * 4 + yh * 2 + c)

    def along(d):
        return dev(z=(z + a * d + NZ) % NZ)

    sibling = dev(c=1 - c)
    partner = dev(yh=1 - yh)
    x_peer = [dev(x=(x + k) % NX) for k in range(1, NX)]
    y_peer = [dev(ylo=(ylo + k) % NYLO) for k in range(1, NYLO)]
    steps = {abs(hop(p, e)) for core in TREE for tree in core for e, p in tree.items()}
    peers = [along(d) for k in sorted(steps) for d in (k, -k)] + [partner, sibling, *x_peer, *y_peer]

    def remote(src, dst, ssem, rsem, to):
        return pltpu.make_async_remote_copy(
            src_ref=src, dst_ref=dst, send_sem=ssem, recv_sem=rsem, device_id=to, device_id_type=MESH
        )

    x_rows = ROWS // NX
    y_rows = ROWS // N_REPLICA
    my_x = pl.ds(pl.multiple_of(x * x_rows, x_rows), x_rows)
    loads = [
        pltpu.make_async_copy(tokens.at[0], tok.at[SLOT[0][OWN, 0]], load_sem.at[0]),
        pltpu.make_async_copy(gate_w, gate_v.at[0], load_sem.at[1]),
        pltpu.make_async_copy(local_up.at[0], up_v.at[0], load_sem.at[2]),
        pltpu.make_async_copy(down_w, down_v.at[0], load_sem.at[3]),
        pltpu.make_async_copy(deltas.at[0, my_x], delta_v, load_sem.at[4]),
        pltpu.make_async_copy(outer_up, outer_v, load_sem.at[5]),
        pltpu.make_async_copy(momentum, mom_v, load_sem.at[6]),
    ]
    barrier = pltpu.get_barrier_semaphore()
    for peer in peers:
        pl.semaphore_signal(barrier, inc=1, device_id=peer, device_id_type=MESH)
    for load in loads:
        load.start()
    pl.semaphore_wait(barrier, len(peers))

    def children(core, side, p):
        return [e for e, parent in TREE[core][side].items() if parent == p]

    def gather_copy(core, side, e, src=None):
        p, s = TREE[core][side][e], SLOT[core][side, e]
        src = tok.at[SLOT[core][side, p]] if src is None else src
        return remote(src, tok.at[s], ag_send.at[s], ag_recv.at[s], along(hop(p, e)))

    def y_tokens(core):
        s = SLOT[core][PAR, 0]
        return remote(tokens.at[0], tok.at[s], y_send.at[0], ag_recv.at[s], partner)

    def reduce_copy(core, side, e):
        p, s = TREE[core][side][e], SLOT[core][side, e]
        src = rs_out if children(core, side, e) else part
        return remote(src.at[s], rs_in.at[s], rs_send.at[s], rs_recv.at[s], along(-hop(p, e)))

    def in_rows(n, size, work):
        def turn(i, carry):
            work(pl.ds(pl.multiple_of(i * size, size), size))
            return carry

        lax.fori_loop(0, n, turn, 0)

    def sum_into(core, side, e, store):
        held = children(core, side, e)
        for child in held:
            reduce_copy(core, side, child).wait_recv()

        def work(rows):
            total = part[SLOT[core][side, e], rows, :].astype(F32)
            for child in held:
                total = total + rs_in[SLOT[core][side, child], rows, :].astype(F32)
            store(rows, total)

        in_rows(4, tok.shape[1] // 4, work)

    y_final = remote(y_out, y_in, y_send.at[1], y_recv.at[0], partner)

    def rows_of(k):
        return pl.ds(pl.multiple_of(k * y_rows, y_rows), y_rows)

    def x_leg(k):
        px = (x + k + 1) % NX
        rows = pl.ds(pl.multiple_of(px * x_rows, x_rows), x_rows)
        return remote(deltas.at[0, rows], x_in.at[k], o_send.at[k], o_recv.at[k], x_peer[k])

    def y_leg(k):
        py = (ylo + k + 1) % NYLO
        return remote(y_mid.at[rows_of(py)], y_sum_in.at[k], o_send.at[3 + k], o_recv.at[3 + k], y_peer[k])

    def y_gather(k):
        rows = rows_of(r)
        return remote(half_all.at[rows], half_all.at[rows], o_send.at[6 + k], o_recv.at[6 + k], y_peer[k])

    def x_gather(k):
        return remote(half_all.at[my_x], half_all.at[my_x], o_send.at[9 + k], o_recv.at[9 + k], x_peer[k])

    def outer(stage):
        if stage == 2:
            loads[4].wait()
            for k in range(3):
                x_leg(k).wait_recv()

            def work(rows):
                total = delta_v[rows, :].astype(F32)
                for k in range(3):
                    total = total + x_in[k, rows, :].astype(F32)
                y_mid[rows, :] = total.astype(BF16)

            in_rows(4, x_rows // 4, work)
            for k in range(3):
                y_leg(k).start()
        elif stage == 3:
            loads[5].wait()
            loads[6].wait()
            total = y_mid[rows_of(ylo), :].astype(F32)
            for k in range(3):
                y_leg(k).wait_recv()
                total = total + y_sum_in[k].astype(F32)
            grad = total / N_REPLICA
            nm = momentum_coef * mom_v[...] + grad
            no = outer_v[...] - outer_rate * (grad + momentum_coef * nm)
            nm_v[...] = nm
            no_v[...] = no
            half_all[rows_of(r), :] = no.astype(BF16)
            for k in range(3):
                y_gather(k).start()
        elif stage == 4:
            for k in range(3):
                y_gather(k).wait_recv()
            for k in range(3):
                x_gather(k).start()
        else:
            for k in range(3):
                x_gather(k).wait_recv()

            def work(rows):
                merged = mix_weight * up_v[0, rows, :].astype(F32) + (1.0 - mix_weight) * half_all[rows, :].astype(F32)
                merged_v[rows, :] = merged.astype(BF16)

            in_rows(16, ROWS // 16, work)

    weights = [
        remote(src, dst.at[1], w_send.at[k], w_recv.at[k], sibling)
        for k, (src, dst) in enumerate(((gate_w, gate_v), (local_up.at[0], up_v), (down_w, down_v)))
    ]

    def sent_all(core, held, sem):
        first, second = sorted((SLOT[core][OWN, 0], SLOT[core][PAR, 0]))

        def turn(s, carry):
            remote(held.at[s], held.at[s], sem.at[s], sem.at[s], partner).wait_send()
            return carry

        for low, high in ((0, first), (first + 1, second), (second + 1, N_SLOT)):
            if low < high:
                lax.fori_loop(low, high, turn, 0)

    def wait_sends(core, stage):
        if stage == 0:
            for weight in weights:
                weight.wait_send()
            y_tokens(core).wait_send()
            sent_all(core, tok, ag_send)
            for k in range(3):
                x_leg(k).wait_send()
                y_leg(k).wait_send()
        elif stage == 1:
            for k in range(3):
                y_gather(k).wait_send()
        else:
            for k in range(3):
                x_gather(k).wait_send()
            sent_all(core, part, rs_send)
            y_final.wait_send()

    def act(core, kind, *what):
        if kind == "g":
            side, e = what
            copy = gather_copy(core, side, e) if e else y_tokens(core)
            copy.wait_recv()
            for child in children(core, side, e):
                gather_copy(core, side, child).start()
        elif kind == "r":
            side, e = what
            if children(core, side, e):


                def store(rows, total):
                    rs_out[SLOT[core][side, e], rows, :] = total.astype(BF16)

                sum_into(core, side, e, store)
            reduce_copy(core, side, e).start()
        elif kind == "f":
            if what[0] == PAR:

                def store(rows, total):
                    y_out[rows, :] = total.astype(BF16)

                sum_into(core, PAR, 0, store)
                y_final.start()
            else:

                def store(rows, total):
                    out_v[rows, :] = (total + y_in[rows, :].astype(F32)).astype(BF16)

                y_final.wait_recv()
                sum_into(core, OWN, 0, store)
        elif kind == "o":
            outer(what[0])
        else:
            wait_sends(core, what[0])

    for core in (0, 1):

        @pl.when(c == core)
        def _():
            for child in children(core, OWN, 0):
                gather_copy(core, OWN, child, tokens.at[0]).start()
            y_tokens(core).start()

    for weight in weights:
        weight.start()
    for k in range(3):
        x_leg(k).start()

    blk, width = tok.shape[1], gate_v.shape[2]

    def compute(i, h):
        rows = tok[pl.ds(2 * i, 2)].reshape(2 * blk, ROWS)
        total = jnp.zeros((2 * blk, ROWS), F32)
        for start in range(0, width, 256):
            cols = slice(start, min(start + 256, width))
            gate = jnp.dot(rows, gate_v[h, :, cols], preferred_element_type=F32)
            upper = jnp.dot(rows, up_v[h, :, cols], preferred_element_type=F32)
            hidden = ((gate + gate * jnp.tanh(0.5 * gate)) * upper).astype(BF16)
            total = total + jnp.dot(hidden, down_v[h, cols, :], preferred_element_type=F32)

        @pl.when(h == 0)
        def _():
            acc[...] = total

        @pl.when(h == 1)
        def _():
            both = (acc[...] + total) * (0.5 * ROWS ** -0.5)
            part[pl.ds(2 * i, 2)] = both.astype(BF16).reshape(2, blk, ROWS)

    def each(todo):
        for core in (0, 1):
            if todo[core]:

                @pl.when(c == core)
                def _():
                    for what in todo[core]:
                        act(core, *what)

    def prepare(at):
        each([BEFORE[core][at] for core in (0, 1)])
        if at == 0:
            for load in loads[:4]:
                load.wait()
        if at == 1:
            for weight in weights:
                weight.wait_recv()

    def dispatch(u, low, high):
        if high - low == 1:
            prepare(low)
            return
        middle = (low + high) // 2
        lax.cond(u < middle, lambda: dispatch(u, low, middle), lambda: dispatch(u, middle, high))

    def unit(u, carry):
        dispatch(u, 0, N_SLOT)
        compute(u // 2, u % 2)
        return carry

    lax.fori_loop(0, N_SLOT, unit, 0)
    each(AFTER)


def store_kernel(*refs):
    n = (len(refs) - 1) // 2
    copies = [pltpu.make_async_copy(src, dst, refs[-1].at[k]) for k, (src, dst) in enumerate(zip(refs[:n], refs[n:-1]))]
    for copy in copies:
        copy.start()
    for copy in copies:
        copy.wait()


def body(tokens, gate_weight, down_weight, local_up, deltas, outer_up, momentum):
    blk, rows = tokens.shape[1:]
    width = gate_weight.shape[1]
    share = outer_up.shape[0]
    dma = pltpu.SemaphoreType.DMA
    outs = (
        ((blk, rows), BF16, tokens.shape),
        ((ROWS, width), BF16, local_up.shape),
        ((share, width), F32, outer_up.shape),
        ((share, width), F32, momentum.shape),
    )
    args = [
        pltpu.with_memory_space_constraint(arg, pltpu.HBM)
        for arg in (tokens, gate_weight, down_weight, local_up, deltas, outer_up, momentum)
    ]
    held = pl.pallas_call(
        kernel,
        out_shape=tuple(pltpu.VMEM(shape, kind) for shape, kind, _ in outs),
        in_specs=[pl.BlockSpec(memory_space=pltpu.HBM)] * 7,
        out_specs=[pl.BlockSpec(memory_space=pltpu.VMEM)] * 4,
        scratch_shapes=[
            pltpu.VMEM((N_SLOT, blk, rows), BF16),
            pltpu.VMEM((2, ROWS, width), BF16),
            pltpu.VMEM((2, ROWS, width), BF16),
            pltpu.VMEM((2, width, ROWS), BF16),
            pltpu.VMEM((ROWS // NX, width), BF16),
            pltpu.VMEM((share, width), F32),
            pltpu.VMEM((share, width), F32),
            pltpu.VMEM((N_SLOT, blk, rows), BF16),
            pltpu.VMEM((2 * blk, rows), F32),
            pltpu.VMEM((N_SLOT, blk, rows), BF16),
            pltpu.VMEM((N_SLOT, blk, rows), BF16),
            pltpu.VMEM((blk, rows), BF16),
            pltpu.VMEM((blk, rows), BF16),
            pltpu.VMEM((NX - 1, ROWS // NX, width), BF16),
            pltpu.VMEM((ROWS // NX, width), BF16),
            pltpu.VMEM((NYLO - 1, share, width), BF16),
            pltpu.VMEM((ROWS, width), BF16),
            dma((7,)),
            dma((3,)),
            dma((3,)),
            dma((N_SLOT,)),
            dma((N_SLOT,)),
            dma((N_SLOT,)),
            dma((N_SLOT,)),
            dma((2,)),
            dma((1,)),
            dma((12,)),
            dma((12,)),
        ],
        compiler_params=pltpu.CompilerParams(
            collective_id=0, has_side_effects=True, vmem_limit_bytes=32 * 1024 * 1024
        ),
        cost_estimate=pl.CostEstimate(flops=5_700_000_000, bytes_accessed=3_000_000, transcendentals=3_700_000),
    )(*args)
    inner_out, merged_up, new_outer, new_momentum = pl.pallas_call(
        store_kernel,
        out_shape=tuple(jax.ShapeDtypeStruct(shape, kind) for shape, kind, _ in outs),
        in_specs=[pl.BlockSpec(memory_space=pltpu.VMEM)] * 4,
        out_specs=[pl.BlockSpec(memory_space=pl.ANY)] * 4,
        scratch_shapes=[dma((4,))],
        compiler_params=pltpu.CompilerParams(vmem_limit_bytes=1024 * 1024),
    )(*[pltpu.with_memory_space_constraint(part, pltpu.VMEM) for part in held])
    return inner_out[None], merged_up[None], new_outer, new_momentum


def solution(mesh):
    placed = (
        P("replica", "fsdp", None),
        P(None, "fsdp"),
        P("fsdp", None),
        P("replica", None, "fsdp"),
        P("replica", None, "fsdp"),
        P("replica", "fsdp"),
        P("replica", "fsdp"),
    )
    return jax.shard_map(
        body,
        mesh=mesh,
        in_specs=placed,
        out_specs=(
            P("replica", "fsdp", None),
            P("replica", None, "fsdp"),
            P("replica", "fsdp"),
            P("replica", "fsdp"),
        ),
        check_vma=False,
    )
```

```python
import jax
import jax.numpy as jnp
from jax import lax
from jax.experimental import pallas as pl
from jax.experimental.pallas import tpu as pltpu
from jax.sharding import PartitionSpec as P

MESH = pl.DeviceIdType.MESH
BF16, F32 = jnp.bfloat16, jnp.float32

NX, NYLO, NZ = 4, 4, 8
N_REPLICA = NX * NYLO
ROWS = 256

outer_rate = 0.7
momentum_coef = 0.9
mix_weight = 0.5

OWN, PAR = 0, 1


def hop(p, e):
    d = (e - p) % NZ
    return d - NZ if d > NZ // 2 else d


TREE = (
    (
        {1: 0, 2: 1, 3: 2, 4: 2, -1: 0, -2: -1, -3: -2},
        {1: 0, 2: 0, 3: 2, 4: 2, -1: 0, -2: 0, -3: -2},
    ),
    (
        {1: 0, 2: 1, 3: 2, 4: 3, -1: 0, -2: -1, -3: -2},
        {1: 0, 2: 0, 3: 2, 4: 2, -1: 0, -2: 0, -3: -2},
    ),
)
PAIRS = (
    (
        ((0, 0), (0, 1)),
        ((0, -1), (1, 0)),
        ((0, 2), (0, -2)),
        ((1, 1), (1, -1)),
        ((1, 2), (1, -2)),
        ((0, 3), (0, -3)),
        ((1, 4), (1, 3)),
        ((0, 4), (1, -3)),
    ),
    (
        ((0, 0), (0, 1)),
        ((0, -1), (1, 0)),
        ((0, 2), (0, -2)),
        ((1, 1), (1, -1)),
        ((1, 2), (1, -2)),
        ((0, 3), (0, -3)),
        ((1, 4), (1, 3)),
        ((0, 4), (1, -3)),
    ),
)
SLOT = [{block: 2 * i + k for i, pair in enumerate(pairs) for k, block in enumerate(pair)} for pairs in PAIRS]
N_SLOT = len(SLOT[0])

BEFORE = (
    (
        (("g", 0, 1), ("g", 0, -1),),
        (),
        (("g", 1, 0),),
        (("g", 0, 2),),
        (("g", 0, -2),),
        (),
        (("g", 1, 1), ("o", 2), ("g", 1, 2), ("g", 1, -1),),
        (),
        (("g", 1, -2), ("r", 1, 1), ("r", 1, -1),),
        (("g", 0, 3),),
        (("g", 0, 4), ("g", 0, -3),),
        (("g", 1, 3), ("o", 3),),
        (("r", 0, 3), ("g", 1, 4), ("r", 0, -3),),
        (("g", 1, -3),),
        (("r", 1, 4), ("r", 1, 3),),
        (),
    ),
    (
        (("g", 0, 1), ("g", 0, -1), ("g", 1, 0),),
        (),
        (),
        (),
        (("g", 0, 2), ("g", 0, -2),),
        (("o", 2),),
        (("g", 1, 1), ("g", 1, 2), ("g", 1, -1),),
        (),
        (("g", 1, -2),),
        (),
        (("g", 0, 3), ("r", 1, 1), ("r", 1, -1), ("g", 0, -3),),
        (),
        (("r", 0, -3), ("o", 3), ("g", 1, 3), ("g", 1, 4),),
        (),
        (("r", 1, 4), ("g", 1, -3), ("g", 0, 4),),
        (),
    ),
)
AFTER = (
    (
        ("r", 1, -3),
        ("r", 0, 4),
        ("r", 0, -2),
        ("o", 4),
        ("r", 1, 2),
        ("w", 0),
        ("r", 1, -2),
        ("r", 0, 2),
        ("r", 0, -1),
        ("f", 1),
        ("r", 0, 1),
        ("o", 5),
        ("w", 1),
        ("w", 2),
        ("f", 0),
    ),
    (
        ("r", 0, 4),
        ("r", 1, 3),
        ("r", 1, -3),
        ("r", 0, -2),
        ("r", 0, 3),
        ("r", 1, 2),
        ("o", 4),
        ("w", 0),
        ("r", 1, -2),
        ("f", 1),
        ("r", 0, 2),
        ("r", 0, -1),
        ("r", 0, 1),
        ("o", 5),
        ("w", 1),
        ("w", 2),
        ("f", 0),
    ),
)


def kernel(
    tokens, gate_w, down_w, local_up, deltas, outer_up, momentum,
    out_v, merged_v, no_v, nm_v,
    tok, gate_v, up_v, down_v, delta_v, outer_v, mom_v,
    part, acc, rs_in, rs_out, y_out, y_in,
    x_in, y_mid, y_sum_in, half_all,
    load_sem, w_send, w_recv, ag_send, ag_recv, rs_send, rs_recv, y_send, y_recv, o_send, o_recv,
):
    r, f = lax.axis_index("replica"), lax.axis_index("fsdp")
    x, ylo = r // NYLO, r % NYLO
    z, yh, c = f // 4, (f // 2) % 2, f % 2
    a = 1 - 2 * c

    def dev(x=x, ylo=ylo, z=z, yh=yh, c=c):
        return (x * NYLO + ylo, z * 4 + yh * 2 + c)

    def along(d):
        return dev(z=(z + a * d + NZ) % NZ)

    sibling = dev(c=1 - c)
    partner = dev(yh=1 - yh)
    x_peer = [dev(x=(x + k) % NX) for k in range(1, NX)]
    y_peer = [dev(ylo=(ylo + k) % NYLO) for k in range(1, NYLO)]
    steps = {abs(hop(p, e)) for core in TREE for tree in core for e, p in tree.items()}
    peers = [along(d) for k in sorted(steps) for d in (k, -k)] + [partner, sibling, *x_peer, *y_peer]

    def remote(src, dst, ssem, rsem, to):
        return pltpu.make_async_remote_copy(
            src_ref=src, dst_ref=dst, send_sem=ssem, recv_sem=rsem, device_id=to, device_id_type=MESH
        )

    x_rows = ROWS // NX
    y_rows = ROWS // N_REPLICA
    my_x = pl.ds(pl.multiple_of(x * x_rows, x_rows), x_rows)
    loads = [
        pltpu.make_async_copy(tokens.at[0], tok.at[SLOT[0][OWN, 0]], load_sem.at[0]),
        pltpu.make_async_copy(gate_w, gate_v.at[0], load_sem.at[1]),
        pltpu.make_async_copy(local_up.at[0], up_v.at[0], load_sem.at[2]),
        pltpu.make_async_copy(down_w, down_v.at[0], load_sem.at[3]),
        pltpu.make_async_copy(deltas.at[0, my_x], delta_v, load_sem.at[4]),
        pltpu.make_async_copy(outer_up, outer_v, load_sem.at[5]),
        pltpu.make_async_copy(momentum, mom_v, load_sem.at[6]),
    ]
    barrier = pltpu.get_barrier_semaphore()
    for peer in peers:
        pl.semaphore_signal(barrier, inc=1, device_id=peer, device_id_type=MESH)
    for load in loads:
        load.start()
    pl.semaphore_wait(barrier, len(peers))

    def children(core, side, p):
        return [e for e, parent in TREE[core][side].items() if parent == p]

    def gather_copy(core, side, e, src=None):
        p, s = TREE[core][side][e], SLOT[core][side, e]
        src = tok.at[SLOT[core][side, p]] if src is None else src
        return remote(src, tok.at[s], ag_send.at[s], ag_recv.at[s], along(hop(p, e)))

    def y_tokens(core):
        s = SLOT[core][PAR, 0]
        return remote(tokens.at[0], tok.at[s], y_send.at[0], ag_recv.at[s], partner)

    def reduce_copy(core, side, e):
        p, s = TREE[core][side][e], SLOT[core][side, e]
        src = rs_out if children(core, side, e) else part
        return remote(src.at[s], rs_in.at[s], rs_send.at[s], rs_recv.at[s], along(-hop(p, e)))

    def in_rows(n, size, work):
        def turn(i, carry):
            work(pl.ds(pl.multiple_of(i * size, size), size))
            return carry

        lax.fori_loop(0, n, turn, 0)

    def sum_into(core, side, e, store):
        held = children(core, side, e)
        for child in held:
            reduce_copy(core, side, child).wait_recv()

        def work(rows):
            total = part[SLOT[core][side, e], rows, :].astype(F32)
            for child in held:
                total = total + rs_in[SLOT[core][side, child], rows, :].astype(F32)
            store(rows, total)

        in_rows(4, tok.shape[1] // 4, work)

    y_final = remote(y_out, y_in, y_send.at[1], y_recv.at[0], partner)

    def rows_of(k):
        return pl.ds(pl.multiple_of(k * y_rows, y_rows), y_rows)

    def x_leg(k):
        px = (x + k + 1) % NX
        rows = pl.ds(pl.multiple_of(px * x_rows, x_rows), x_rows)
        return remote(deltas.at[0, rows], x_in.at[k], o_send.at[k], o_recv.at[k], x_peer[k])

    def y_leg(k):
        py = (ylo + k + 1) % NYLO
        return remote(y_mid.at[rows_of(py)], y_sum_in.at[k], o_send.at[3 + k], o_recv.at[3 + k], y_peer[k])

    def y_gather(k):
        rows = rows_of(r)
        return remote(half_all.at[rows], half_all.at[rows], o_send.at[6 + k], o_recv.at[6 + k], y_peer[k])

    def x_gather(k):
        return remote(half_all.at[my_x], half_all.at[my_x], o_send.at[9 + k], o_recv.at[9 + k], x_peer[k])

    def outer(stage):
        if stage == 2:
            loads[4].wait()
            for k in range(3):
                x_leg(k).wait_recv()

            def work(rows):
                total = delta_v[rows, :].astype(F32)
                for k in range(3):
                    total = total + x_in[k, rows, :].astype(F32)
                y_mid[rows, :] = total.astype(BF16)

            in_rows(4, x_rows // 4, work)
            for k in range(3):
                y_leg(k).start()
        elif stage == 3:
            loads[5].wait()
            loads[6].wait()
            total = y_mid[rows_of(ylo), :].astype(F32)
            for k in range(3):
                y_leg(k).wait_recv()
                total = total + y_sum_in[k].astype(F32)
            grad = total / N_REPLICA
            nm = momentum_coef * mom_v[...] + grad
            no = outer_v[...] - outer_rate * (grad + momentum_coef * nm)
            nm_v[...] = nm
            no_v[...] = no
            half_all[rows_of(r), :] = no.astype(BF16)
            for k in range(3):
                y_gather(k).start()
        elif stage == 4:
            for k in range(3):
                y_gather(k).wait_recv()
            for k in range(3):
                x_gather(k).start()
        else:
            for k in range(3):
                x_gather(k).wait_recv()

            def work(rows):
                merged = mix_weight * up_v[0, rows, :].astype(F32) + (1.0 - mix_weight) * half_all[rows, :].astype(F32)
                merged_v[rows, :] = merged.astype(BF16)

            in_rows(16, ROWS // 16, work)

    weights = [
        remote(src, dst.at[1], w_send.at[k], w_recv.at[k], sibling)
        for k, (src, dst) in enumerate(((gate_w, gate_v), (local_up.at[0], up_v), (down_w, down_v)))
    ]

    def sent_all(core, held, sem):
        first, second = sorted((SLOT[core][OWN, 0], SLOT[core][PAR, 0]))

        def turn(s, carry):
            remote(held.at[s], held.at[s], sem.at[s], sem.at[s], partner).wait_send()
            return carry

        for low, high in ((0, first), (first + 1, second), (second + 1, N_SLOT)):
            if low < high:
                lax.fori_loop(low, high, turn, 0)

    def wait_sends(core, stage):
        if stage == 0:
            for weight in weights:
                weight.wait_send()
            y_tokens(core).wait_send()
            sent_all(core, tok, ag_send)
            for k in range(3):
                x_leg(k).wait_send()
                y_leg(k).wait_send()
        elif stage == 1:
            for k in range(3):
                y_gather(k).wait_send()
        else:
            for k in range(3):
                x_gather(k).wait_send()
            sent_all(core, part, rs_send)
            y_final.wait_send()

    def act(core, kind, *what):
        if kind == "g":
            side, e = what
            copy = gather_copy(core, side, e) if e else y_tokens(core)
            copy.wait_recv()
            for child in children(core, side, e):
                gather_copy(core, side, child).start()
        elif kind == "r":
            side, e = what
            if children(core, side, e):


                def store(rows, total):
                    rs_out[SLOT[core][side, e], rows, :] = total.astype(BF16)

                sum_into(core, side, e, store)
            reduce_copy(core, side, e).start()
        elif kind == "f":
            if what[0] == PAR:

                def store(rows, total):
                    y_out[rows, :] = total.astype(BF16)

                sum_into(core, PAR, 0, store)
                y_final.start()
            else:

                def store(rows, total):
                    out_v[rows, :] = (total + y_in[rows, :].astype(F32)).astype(BF16)

                y_final.wait_recv()
                sum_into(core, OWN, 0, store)
        elif kind == "o":
            outer(what[0])
        else:
            wait_sends(core, what[0])

    for core in (0, 1):

        @pl.when(c == core)
        def _():
            for child in children(core, OWN, 0):
                gather_copy(core, OWN, child, tokens.at[0]).start()
            y_tokens(core).start()

    for weight in weights:
        weight.start()
    for k in range(3):
        x_leg(k).start()

    blk, width = tok.shape[1], gate_v.shape[2]

    def compute(i, h):
        rows = tok[pl.ds(2 * i, 2)].reshape(2 * blk, ROWS)
        total = jnp.zeros((2 * blk, ROWS), F32)
        for start in range(0, width, 256):
            cols = slice(start, min(start + 256, width))
            gate = jnp.dot(rows, gate_v[h, :, cols], preferred_element_type=F32)
            upper = jnp.dot(rows, up_v[h, :, cols], preferred_element_type=F32)
            hidden = ((gate + gate * jnp.tanh(0.5 * gate)) * upper).astype(BF16)
            total = total + jnp.dot(hidden, down_v[h, cols, :], preferred_element_type=F32)

        @pl.when(h == 0)
        def _():
            acc[...] = total

        @pl.when(h == 1)
        def _():
            both = (acc[...] + total) * (0.5 * ROWS ** -0.5)
            part[pl.ds(2 * i, 2)] = both.astype(BF16).reshape(2, blk, ROWS)

    def each(todo):
        for core in (0, 1):
            if todo[core]:

                @pl.when(c == core)
                def _():
                    for what in todo[core]:
                        act(core, *what)

    def prepare(at):
        each([BEFORE[core][at] for core in (0, 1)])
        if at == 0:
            for load in loads[:4]:
                load.wait()
        if at == 1:
            for weight in weights:
                weight.wait_recv()

    def dispatch(u, low, high):
        if high - low == 1:
            prepare(low)
            return
        middle = (low + high) // 2
        lax.cond(u < middle, lambda: dispatch(u, low, middle), lambda: dispatch(u, middle, high))

    def unit(u, carry):
        dispatch(u, 0, N_SLOT)
        compute(u // 2, u % 2)
        return carry

    lax.fori_loop(0, N_SLOT, unit, 0)
    each(AFTER)


def store_kernel(*refs):
    n = (len(refs) - 1) // 2
    copies = [pltpu.make_async_copy(src, dst, refs[-1].at[k]) for k, (src, dst) in enumerate(zip(refs[:n], refs[n:-1]))]
    for copy in copies:
        copy.start()
    for copy in copies:
        copy.wait()


def body(tokens, gate_weight, down_weight, local_up, deltas, outer_up, momentum):
    blk, rows = tokens.shape[1:]
    width = gate_weight.shape[1]
    share = outer_up.shape[0]
    dma = pltpu.SemaphoreType.DMA
    outs = (
        ((blk, rows), BF16, tokens.shape),
        ((ROWS, width), BF16, local_up.shape),
        ((share, width), F32, outer_up.shape),
        ((share, width), F32, momentum.shape),
    )
    args = [
        pltpu.with_memory_space_constraint(arg, pltpu.HBM)
        for arg in (tokens, gate_weight, down_weight, local_up, deltas, outer_up, momentum)
    ]
    held = pl.pallas_call(
        kernel,
        out_shape=tuple(pltpu.VMEM(shape, kind) for shape, kind, _ in outs),
        in_specs=[pl.BlockSpec(memory_space=pltpu.HBM)] * 7,
        out_specs=[pl.BlockSpec(memory_space=pltpu.VMEM)] * 4,
        scratch_shapes=[
            pltpu.VMEM((N_SLOT, blk, rows), BF16),
            pltpu.VMEM((2, ROWS, width), BF16),
            pltpu.VMEM((2, ROWS, width), BF16),
            pltpu.VMEM((2, width, ROWS), BF16),
            pltpu.VMEM((ROWS // NX, width), BF16),
            pltpu.VMEM((share, width), F32),
            pltpu.VMEM((share, width), F32),
            pltpu.VMEM((N_SLOT, blk, rows), BF16),
            pltpu.VMEM((2 * blk, rows), F32),
            pltpu.VMEM((N_SLOT, blk, rows), BF16),
            pltpu.VMEM((N_SLOT, blk, rows), BF16),
            pltpu.VMEM((blk, rows), BF16),
            pltpu.VMEM((blk, rows), BF16),
            pltpu.VMEM((NX - 1, ROWS // NX, width), BF16),
            pltpu.VMEM((ROWS // NX, width), BF16),
            pltpu.VMEM((NYLO - 1, share, width), BF16),
            pltpu.VMEM((ROWS, width), BF16),
            dma((7,)),
            dma((3,)),
            dma((3,)),
            dma((N_SLOT,)),
            dma((N_SLOT,)),
            dma((N_SLOT,)),
            dma((N_SLOT,)),
            dma((2,)),
            dma((1,)),
            dma((12,)),
            dma((12,)),
        ],
        compiler_params=pltpu.CompilerParams(
            collective_id=0, has_side_effects=True, vmem_limit_bytes=32 * 1024 * 1024
        ),
        cost_estimate=pl.CostEstimate(flops=5_700_000_000, bytes_accessed=3_000_000, transcendentals=3_700_000),
    )(*args)
    inner_out, merged_up, new_outer, new_momentum = pl.pallas_call(
        store_kernel,
        out_shape=tuple(jax.ShapeDtypeStruct(shape, kind) for shape, kind, _ in outs),
        in_specs=[pl.BlockSpec(memory_space=pltpu.VMEM)] * 4,
        out_specs=[pl.BlockSpec(memory_space=pl.ANY)] * 4,
        scratch_shapes=[dma((4,))],
        compiler_params=pltpu.CompilerParams(vmem_limit_bytes=1024 * 1024),
    )(*[pltpu.with_memory_space_constraint(part, pltpu.VMEM) for part in held])
    return inner_out[None], merged_up[None], new_outer, new_momentum


def solution(mesh):
    placed = (
        P("replica", "fsdp", None),
        P(None, "fsdp"),
        P("fsdp", None),
        P("replica", None, "fsdp"),
        P("replica", None, "fsdp"),
        P("replica", "fsdp"),
        P("replica", "fsdp"),
    )
    return jax.shard_map(
        body,
        mesh=mesh,
        in_specs=placed,
        out_specs=(
            P("replica", "fsdp", None),
            P("replica", None, "fsdp"),
            P("replica", "fsdp"),
            P("replica", "fsdp"),
        ),
        check_vma=False,
    )
```
